32 devices in a mesh: group: 1, expert: 32 (over z, y, x, core).
Axes of the slice: x: 2, y: 2, z: 4, core: 2. Of those that a mesh axis runs over, the one named last changes fastest.
Arguments:
- hidden_in: bfloat16 [256, 7168], P(('group', 'expert')), may hold values from -1.75 to 1.75
- q_latent: bfloat16 [256, 128, 512], P(('group', 'expert')), may hold values from -4 to 4
- q_rope: bfloat16 [256, 8192], P(('group', 'expert')), may hold values from -125 to 125
- cache_latent: bfloat16 [256, 256, 512], P(('group', 'expert')), may hold values from -6 to 6
- cache_rope: bfloat16 [256, 64, 256], P(('group', 'expert')), may hold values from -4 to 4
- lengths: int32 [256], P(('group', 'expert')), may hold values from 2 to 256, as said below
- value_up_weight: bfloat16 [128, 512, 128], P('expert'), may hold values from -0.25 to 0.25
- out_weight: bfloat16 [16384, 7168], P('expert'), may hold values from -0.046875 to 0.046875
- norm_gain: bfloat16 [7168], replicated, may hold values from 0.099609375 to 1.8984375
- route_ids: int32 [256, 4], P(('group', 'expert')), may hold values from 0 to 3, all different within a row; in each aligned block of 8 rows (0 to 7, 8 to 15, ...) at most 8 rows name the same one
- route_logits: float32 [256, 4], P(('group', 'expert')), may hold values from -12 to 12
- gate_weight: bfloat16 [32, 7168, 128], P('expert'), may hold values from -0.0625 to 0.0625
- up_weight: bfloat16 [32, 7168, 128], P('expert'), may hold values from -0.0625 to 0.0625
- down_projection_weight: bfloat16 [32, 128, 7168], P('expert'), may hold values from -0.1875 to 0.1875
Outputs:
- layer_out: bfloat16 [256, 7168], P(('group', 'expert'))
The draws below stay inside these ranges and needn't reach their ends.
Inputs may be any that keep to these rules, and one draw needn't show every extreme that they name: `route_ids`: each row names 4 different experts; among the 8 tokens of one device no expert is named more than 8 times, a bound that some block reaches. `lengths`: some token has exactly 256 valid rows.
All inputs are finite; a program needn't handle non-finite values.
Results may differ from the reference program's by a relative error of at most 0.014.
Values may be sent and summed in bfloat16 or wider, within the bound.
No kernel may reach another device: no remote copies, remote signals or barrier semaphores. Data moves between devices by JAX's collectives and lax.ppermute only.
A program may use at most 256 MiB of HBM per device.

```python
import math
import jax
import jax.numpy as jnp
import numpy as np
from jax import lax

D = 7168
HEADS = 128
KV_RANK = 512
RDIM = 64
V_DIM = 128
FF = 1024
SHARDS = 8
T_DEV = 8
TOP = 4
L = 256
EXPERTS = 4
FF_DEV = 128
CAP = 8
TOKENS = 256
N_EXPERT = 32


def draw_q_latent(key, part):
    key = jax.random.fold_in(key, 5)
    values = jnp.clip(jax.random.normal(key, (TOKENS, HEADS, KV_RANK)), -4.0, 4.0)
    return values.astype(jnp.bfloat16)


def draw_q_rope(key, part):
    key = jax.random.fold_in(key, 7)
    values = jnp.clip(jax.random.normal(key, (TOKENS, HEADS, RDIM)), -4.0, 4.0)
    return values.reshape(TOKENS, HEADS * RDIM).astype(jnp.bfloat16)


def draw_cache_rope(key, part):
    key = jax.random.fold_in(key, 9)
    values = jnp.clip(jax.random.normal(key, (TOKENS, L, RDIM)), -4.0, 4.0)
    return jnp.transpose(values, (0, 2, 1)).astype(jnp.bfloat16)


def draw_lengths(key, part):
    key = jax.random.fold_in(key, 3)
    subkeys = jax.random.split(key, 2)
    groups = TOKENS // T_DEV
    ceilings = jax.random.randint(subkeys[0], (groups, 1), L // 8, L + 1)
    raw_draws = jax.random.randint(subkeys[1], (groups, T_DEV), 0, 1 << 20)
    lengths_all = 2 + raw_draws % (ceilings - 1)
    lengths_all = lengths_all.reshape(TOKENS).at[0].set(L)
    return lengths_all.astype(jnp.int32)


def block_scale(rng, shape, shards, least, top_value):
    def one(axis_at, parts):
        draws = jax.random.uniform(jax.random.fold_in(jax.random.fold_in(rng, 6), axis_at), (parts,), jnp.float32, least / len(shards), top_value / len(shards))
        return jnp.repeat(jnp.exp(draws), shape[axis_at] // parts).reshape((-1,) + (1,) * (len(shape) - axis_at - 1))

    loudness = one(*shards[0])
    for cut in shards[1:]:
        loudness = loudness * one(*cut)
    return loudness


def deal_out(own_key, own, number, rows, number_of, top, most, skew):
    sequence = jax.random.permutation(own_key, number_of)
    heavy_load, common = shares(number_of, rows * top, most, skew, True), shares(number_of, rows * top, most, skew, False)
    places = jnp.arange(number_of)

    def named(sizes, rotation):
        used = int((sizes > 0).sum())
        fixed = max(1, used // 4)
        moved = fixed + (places - fixed + rotation * (used - fixed)) % max(1, number_of - fixed)
        return jnp.zeros((number_of,), jnp.int32).at[sequence[jnp.where(places < fixed, places, moved)]].set(jnp.asarray(sizes, jnp.int32))

    sizes = jnp.where(number % 4 == 0, named(heavy_load, number // 4), named(common, number - number // 4 - 1))
    mixed = jax.random.permutation(jax.random.fold_in(own, 3), number_of)
    source_of, taker = mixed[0:number_of // 2 * 2:2], mixed[1:number_of // 2 * 2:2]
    slack = jnp.minimum(sizes[source_of] - 1, most - sizes[taker]) // 2
    slack = jnp.where((source_of == sequence[0]) | (taker == sequence[0]) | (sizes[taker] == 0), 0, jnp.maximum(slack, 0))
    moved = jax.random.randint(jax.random.fold_in(own, 4), (number_of // 2,), 0, 1 << 20) % (slack + 1)
    sizes = sizes.at[source_of].add(-moved).at[taker].add(moved)
    labels = jnp.searchsorted(jnp.cumsum(sizes), jnp.arange(rows * top), side="right").astype(jnp.int32)
    listing = labels.reshape(top, rows).T
    listing = listing[jax.random.permutation(jax.random.fold_in(own, 1), rows)]
    rotation = jax.random.randint(jax.random.fold_in(own, 2), (rows, 1), 0, top)
    return jnp.take_along_axis(listing, (jnp.arange(top)[None, :] + rotation) % top, axis=1)


def shares(amount, total, bound, slope, full):
    portions = [(1 << 20) // math.isqrt(standing ** slope) + 1 for standing in range(1, amount + 1)]
    largest = bound if full else min(bound, max(-(-total // amount), total * portions[0] // sum(portions)))
    least = 1 if total - largest >= amount - 1 else 0
    given, surplus = [largest] + [least] * (amount - 1), total - largest - least * (amount - 1)
    while surplus > 0:
        free = [i for i in range(1, amount) if given[i] < largest] or [i for i in range(1, amount) if given[i] < bound]
        pool, remaining = sum([portions[i] for i in free]), surplus
        for i in free:
            addition = min(bound - given[i], max(1, remaining * portions[i] // pool), surplus)
            given[i] = given[i] + addition
            surplus = surplus - addition
    return np.array(given)


def bell_draw(stream_key, extent, deviation, bound, cuts=(), held_as=jnp.bfloat16):
    drawn = jax.random.normal(stream_key, extent, jnp.float32) * deviation
    if len(cuts) > 0:
        drawn = block_scale(stream_key, extent, cuts, -0.22, 0.18) * drawn
    return jnp.clip(drawn, min=-bound, max=bound).astype(held_as)


def setup_inputs(seed: int = 0, part: int = 0) -> dict:
    seeds = jax.random.split(jax.random.key(seed), 15)
    own_keys = jax.random.split(jax.random.fold_in(seeds[14], part), 15)
    hidden_in = bell_draw(own_keys[0], (TOKENS, D), 0.3, 1.75, ((0, 32),))
    q_latent = draw_q_latent(jax.random.fold_in(jax.random.fold_in(seeds[14], part), 71), part)
    q_rope = draw_q_rope(jax.random.fold_in(jax.random.fold_in(seeds[14], part), 71), part)
    cache_latent = bell_draw(own_keys[3], (TOKENS, L, KV_RANK), 1.0, 6.0, ((0, 32),))
    cache_rope = draw_cache_rope(jax.random.fold_in(jax.random.fold_in(seeds[14], part), 71), part)
    lengths = draw_lengths(jax.random.fold_in(jax.random.fold_in(seeds[14], part), 71), part)
    value_up_weight = bell_draw(seeds[6], (HEADS, KV_RANK, V_DIM), KV_RANK ** -0.5, 0.25, ((0, 32),))
    out_weight = bell_draw(seeds[7], (HEADS * V_DIM, D), (HEADS * V_DIM) ** -0.5, 0.046875, ((0, 32),))
    norm_gain = jnp.clip(1.0 + 0.18 * jax.random.normal(seeds[8], (D,), jnp.float32), 0.099609375, 1.8984375).astype(jnp.bfloat16)
    route_ids_keys = jax.random.split(jax.random.fold_in(own_keys[9], 1), TOKENS // T_DEV)
    route_ids_turns = jax.random.permutation(jax.random.fold_in(own_keys[9], 3), TOKENS // T_DEV)
    route_ids = jax.vmap(lambda own, number: deal_out(jax.random.fold_in(own_keys[9], 2), own, number, T_DEV, EXPERTS, TOP, CAP, 2))(route_ids_keys, route_ids_turns).reshape((TOKENS, TOP))
    route_logits = bell_draw(own_keys[10], (TOKENS, TOP), 2.0, 12.0, ((0, 32),), jnp.float32)
    gate_weight = bell_draw(seeds[11], (EXPERTS * SHARDS, D, FF_DEV), D ** -0.5, 0.0625, ((0, 32),))
    up_weight = bell_draw(seeds[12], (EXPERTS * SHARDS, D, FF_DEV), D ** -0.5, 0.0625, ((0, 32),))
    down_projection_weight = bell_draw(seeds[13], (EXPERTS * SHARDS, FF_DEV, D), FF ** -0.5, 0.1875, ((0, 32),))
    return dict(hidden_in=hidden_in, q_latent=q_latent, q_rope=q_rope, cache_latent=cache_latent, cache_rope=cache_rope, lengths=lengths, value_up_weight=value_up_weight, out_weight=out_weight, norm_gain=norm_gain, route_ids=route_ids, route_logits=route_logits, gate_weight=gate_weight, up_weight=up_weight, down_projection_weight=down_projection_weight)


score_scale = 192.0 ** (-0.5)
epsilon = 1e-06
route_scale = 2.5

def attend_token(inputs):
    query_lat, query_rot, latent_cache_rows, cache_rot, valid_rows = inputs
    scores = jnp.dot(query_lat, latent_cache_rows.T, preferred_element_type=jnp.float32)
    scores = scores + jnp.dot(query_rot.reshape(HEADS, RDIM), cache_rot, preferred_element_type=jnp.float32)
    scores = scores * score_scale
    usable = jnp.arange(L, dtype=jnp.int32) < valid_rows
    scores = jnp.where(usable[None, :], scores, -jnp.inf)
    highest = lax.optimization_barrier(jnp.max(scores, axis=1, keepdims=True))
    expd = jnp.exp(scores - highest)
    attention_probabilities = (expd / lax.optimization_barrier(jnp.sum(expd, axis=1, keepdims=True))).astype(jnp.bfloat16)
    return jnp.dot(attention_probabilities, latent_cache_rows, preferred_element_type=jnp.float32).astype(jnp.bfloat16)

def slot_table(routes):
    flattened = routes.reshape(-1)
    onehot = (flattened[:, None] == jnp.arange(EXPERTS, dtype=jnp.int32)[None, :]).astype(jnp.int32)
    before = jnp.cumsum(onehot, axis=0) - onehot
    ranking = lax.optimization_barrier(jnp.sum(before * onehot, axis=1))
    return (flattened * CAP + ranking).reshape(routes.shape).astype(jnp.int32)

def expert_rows(inputs):
    rows_in, gate_blocks, up_blocks, down_blocks = inputs
    running = jnp.zeros(rows_in.shape, jnp.float32)
    for shard_index in range(SHARDS):
        gate_act = jnp.dot(rows_in, gate_blocks[shard_index], preferred_element_type=jnp.float32)
        up_act = jnp.dot(rows_in, up_blocks[shard_index], preferred_element_type=jnp.float32)
        hidden = (jax.nn.silu(gate_act) * up_act).astype(jnp.bfloat16)
        piece_out = jnp.dot(hidden, down_blocks[shard_index], preferred_element_type=jnp.float32).astype(jnp.bfloat16)
        running = running + piece_out.astype(jnp.float32)
    return running

def reference(hidden_in, q_latent, q_rope, cache_latent, cache_rope, lengths, value_up_weight, out_weight, norm_gain, route_ids, route_logits, gate_weight, up_weight, down_projection_weight):
    latent_context_output = lax.map(attend_token, (q_latent, q_rope, cache_latent, cache_rope, lengths))
    per_head_value_rows = jnp.einsum('bqn,qnz->bqz', latent_context_output.astype(jnp.float32), value_up_weight.astype(jnp.float32)).astype(jnp.bfloat16)
    attn = jnp.dot(per_head_value_rows.reshape(TOKENS, HEADS * V_DIM), out_weight, preferred_element_type=jnp.float32)
    residual = (hidden_in.astype(jnp.float32) + attn).astype(jnp.bfloat16)
    res32 = residual.astype(jnp.float32)
    normed = (res32 * lax.rsqrt(lax.optimization_barrier(jnp.mean(res32 * res32, axis=1, keepdims=True)) + epsilon) * norm_gain.astype(jnp.float32)).astype(jnp.bfloat16)
    sigm = jax.nn.sigmoid(route_logits)
    route_weights = route_scale * sigm / lax.optimization_barrier(jnp.sum(sigm, axis=1, keepdims=True))
    slot_ids = jax.vmap(slot_table)(route_ids.reshape(N_EXPERT, T_DEV, TOP))
    slot_range = jnp.arange(EXPERTS * CAP, dtype=jnp.int32)
    matches = (slot_ids[:, :, :, None] == slot_range[None, None, None, :]).astype(jnp.float32)
    placement = lax.optimization_barrier(jnp.sum(matches, axis=2))
    buffers = jnp.einsum('ntq,ntd->nqd', placement, normed.reshape(N_EXPERT, T_DEV, D).astype(jnp.float32)).astype(jnp.bfloat16)
    per_expert = buffers.reshape(N_EXPERT, EXPERTS, CAP, D).transpose(1, 0, 2, 3).reshape(EXPERTS, N_EXPERT * CAP, D)
    expert_out = lax.map(expert_rows, (per_expert, gate_weight.reshape(EXPERTS, SHARDS, D, FF_DEV), up_weight.reshape(EXPERTS, SHARDS, D, FF_DEV), down_projection_weight.reshape(EXPERTS, SHARDS, FF_DEV, D)))
    expert_out = expert_out.reshape(EXPERTS, N_EXPERT, CAP, D).transpose(1, 0, 2, 3).reshape(N_EXPERT, EXPERTS * CAP, D)
    combiner = lax.optimization_barrier(jnp.sum(route_weights.reshape(N_EXPERT, T_DEV, TOP)[:, :, :, None] * matches, axis=2))
    expert_sum = jnp.einsum('ntq,nqd->ntd', combiner, expert_out, precision=lax.Precision.HIGHEST)
    return (res32 + expert_sum.reshape(TOKENS, D)).astype(jnp.bfloat16)
```

```python
import jax
import jax.numpy as jnp
from jax import lax
from jax.sharding import PartitionSpec as P

SHARDS = 8
LANES = 128


score_scale = 192.0 ** (-0.5)
epsilon = 1e-06
route_scale = 2.5
f32 = jnp.float32
bf16 = jnp.bfloat16


def slot_table(routes, experts, capacity):
    flattened = routes.reshape(-1)
    onehot = (flattened[:, None] == jnp.arange(experts, dtype=jnp.int32)[None, :]).astype(jnp.int32)
    before = jnp.cumsum(onehot, axis=0) - onehot
    ranking = jnp.sum(before * onehot, axis=1)
    return (flattened * capacity + ranking).reshape(routes.shape)


def swap(x, bit, devices):
    return lax.ppermute(x, "expert", [(i, i ^ (1 << bit)) for i in range(devices)])


def pick(x, bits, bit, value):
    return lax.index_in_dim(x, value, bits.index(bit), keepdims=False)


def scatter_sum(partial, order, devices):
    bits = list(range(len(order)))[::-1]
    send = pick(partial, bits, order[0], 1).astype(bf16)
    keep = pick(partial, bits, order[0], 0)
    bits.remove(order[0])
    for step, bit in enumerate(order):
        came = swap(send, bit, devices)
        if step + 1 == len(order):
            return keep.astype(f32) + came.astype(f32)
        after = order[step + 1]
        halves = [
            pick(keep, bits, after, v).astype(f32) + pick(came, bits, after, v).astype(f32)
            for v in (0, 1)
        ]
        bits.remove(after)
        keep, send = halves[0].astype(bf16), halves[1].astype(bf16)


def gather(block, order, devices):
    bits = []
    for bit in order:
        came = swap(block, bit, devices)
        place = len([b for b in bits if b > bit])
        block = jnp.stack([block, came], axis=place)
        bits.insert(place, bit)
    return block


def chain_orders(nbits):
    rest = list(range(1, nbits))
    orders = []
    for first in (0, 1, 2):
        lead = [rest[first], *[b for b in rest[:3] if b != rest[first]]]
        orders.append([0, *lead, *rest[3:]])
    return orders


def cuts(width, chunks):
    tiles = width // LANES
    sizes = [(tiles // chunks + (1 if i < tiles % chunks else 0)) * LANES for i in range(chunks)]
    starts = [sum(sizes[:i]) for i in range(chunks)]
    return list(zip(starts, sizes, strict=True))


def three_parts(x):
    parts = []
    for _ in range(3):
        part = lax.reduce_precision(x, 8, 7)
        parts.append(part.astype(bf16))
        x = x - part
    return parts


def attend(q_latent, q_rope, cache_latent, cache_rope, lengths):
    tokens_here, heads_all, _ = q_latent.shape
    rope_width = cache_rope.shape[1]
    cache_rows = cache_latent.shape[1]
    scores = jnp.einsum("thk,tlk->thl", q_latent, cache_latent, preferred_element_type=f32)
    scores = scores + jnp.einsum(
        "thr,trl->thl",
        q_rope.reshape(tokens_here, heads_all, rope_width),
        cache_rope,
        preferred_element_type=f32,
    )
    scores = scores * score_scale
    usable = jnp.arange(cache_rows, dtype=jnp.int32)[None, :] < lengths[:, None]
    scores = jnp.where(usable[:, None, :], scores, -jnp.inf)
    highest = jnp.max(scores, axis=2, keepdims=True)
    expd = jnp.exp(scores - highest)
    weights = (expd / jnp.sum(expd, axis=2, keepdims=True)).astype(bf16)
    return jnp.einsum("thl,tlk->thk", weights, cache_latent, preferred_element_type=f32).astype(bf16)


def shards(
    hidden_in,
    q_latent,
    q_rope,
    cache_latent,
    cache_rope,
    lengths,
    value_up_weight,
    out_weight,
    norm_gain,
    route_ids,
    route_logits,
    gate_weight,
    up_weight,
    down_projection_weight,
):
    devices = lax.axis_size("expert")
    me = lax.axis_index("expert")
    nbits = devices.bit_length() - 1
    tokens_here = hidden_in.shape[0]
    model_width = hidden_in.shape[1]
    top_count = route_ids.shape[1]
    experts = devices // SHARDS
    orders = chain_orders(nbits)
    chunks = cuts(model_width, len(orders))
    sigm = jax.nn.sigmoid(route_logits)
    route_weights = route_scale * sigm / jnp.sum(sigm, axis=1, keepdims=True)

    latent_out = attend(q_latent, q_rope, cache_latent, cache_rope, lengths)
    by_head = lax.all_to_all(latent_out, "expert", split_axis=1, concat_axis=0, tiled=True)
    head_values = jnp.einsum(
        "aqg,qge->aqe", by_head, value_up_weight, preferred_element_type=f32
    ).astype(bf16)
    rows = devices * tokens_here
    head_values = head_values.reshape(rows, -1)
    at = jnp.arange(rows, dtype=jnp.int32)
    source = (((at // tokens_here) ^ me) * tokens_here) + at % tokens_here
    shuffle = (source[:, None] == at[None, :]).astype(bf16)
    head_values = jnp.dot(shuffle, head_values, preferred_element_type=f32).astype(bf16)
    blocks = (2,) * nbits + (tokens_here,)

    residual = []
    for (start, size), order in zip(chunks, orders, strict=True):
        partial = jnp.dot(
            head_values, out_weight[:, start : start + size], preferred_element_type=f32
        ).reshape(*blocks, size)
        attn = scatter_sum(partial, order, devices)
        residual.append((hidden_in[:, start : start + size].astype(f32) + attn).astype(bf16))

    if experts > top_count:
        return routed(
            jnp.concatenate(residual, axis=1),
            norm_gain,
            route_ids,
            route_weights,
            gate_weight,
            up_weight,
            down_projection_weight,
        )

    chosen = route_ids[:, :, None] == jnp.arange(experts, dtype=jnp.int32)[None, None, :]
    shares = jnp.sum(jnp.where(chosen, route_weights[:, :, None], 0.0), axis=1)
    extra = jnp.concatenate(three_parts(shares), axis=1)
    extra = jnp.pad(extra, ((0, 0), (0, LANES - extra.shape[1])))
    gate_act = jnp.zeros((rows, gate_weight.shape[2]), f32)
    up_act = jnp.zeros((rows, up_weight.shape[2]), f32)
    squares = jnp.zeros((rows, 1), f32)
    for i, ((start, size), order) in enumerate(zip(chunks, orders, strict=True)):
        last = i + 1 == len(chunks)
        block = jnp.concatenate([residual[i], extra], axis=1) if last else residual[i]
        taken = gather(block, order[::-1], devices).reshape(rows, -1)
        if last:
            got = taken[:, size:].astype(f32)
            taken = taken[:, :size]
        wide = taken.astype(f32)
        squares = squares + jnp.sum(wide * wide, axis=1, keepdims=True)
        scaled = (wide * norm_gain[start : start + size].astype(f32)).astype(bf16)
        gate_act = gate_act + jnp.dot(
            scaled, gate_weight[0, start : start + size], preferred_element_type=f32
        )
        up_act = up_act + jnp.dot(
            scaled, up_weight[0, start : start + size], preferred_element_type=f32
        )
    factor = lax.rsqrt(squares / model_width + epsilon)
    own = (jnp.arange(LANES, dtype=jnp.int32) % experts == me // SHARDS) & (
        jnp.arange(LANES, dtype=jnp.int32) < 3 * experts
    )
    share = jnp.sum(jnp.where(own[None, :], got, 0.0), axis=1, keepdims=True)
    hidden = (jax.nn.silu(gate_act * factor) * (up_act * factor) * share).astype(bf16)
    out = []
    for (start, size), order, base in zip(chunks, orders, residual, strict=True):
        piece = jnp.dot(
            hidden, down_projection_weight[0, :, start : start + size], preferred_element_type=f32
        ).reshape(*blocks, size)
        out.append((base.astype(f32) + scatter_sum(piece, order, devices)).astype(bf16))
    return jnp.concatenate(out, axis=1)


def routed(
    residual, norm_gain, route_ids, route_weights, gate_weight, up_weight, down_projection_weight
):
    devices = lax.axis_size("expert")
    tokens_here, model_width = residual.shape
    top_count = route_ids.shape[1]
    experts = devices // SHARDS
    capacity = min(tokens_here, max(2, (tokens_here * top_count + experts - 1) // experts + 1))
    slot_count = experts * capacity
    slot_ids = slot_table(route_ids, experts, capacity)
    slot_range = jnp.arange(slot_count, dtype=jnp.int32)
    res32 = residual.astype(f32)
    normed = (
        res32
        * lax.rsqrt(jnp.mean(res32 * res32, axis=1, keepdims=True) + epsilon)
        * norm_gain.astype(f32)
    ).astype(bf16)
    placement = jnp.sum(
        (slot_ids[:, :, None] == slot_range[None, None, :]).astype(jnp.int32), axis=1
    ).astype(bf16)
    outgoing = jnp.einsum("tq,tw->qw", placement, normed, preferred_element_type=f32).astype(bf16)
    outgoing = jnp.broadcast_to(
        outgoing.reshape(experts, 1, capacity, model_width),
        (experts, SHARDS, capacity, model_width),
    )
    outgoing = outgoing.reshape(devices, capacity, model_width)
    received = lax.all_to_all(outgoing, "expert", split_axis=0, concat_axis=0, tiled=True)
    sources, item_count, feature_count = received.shape
    flattened = received.reshape(sources * item_count, feature_count)
    gate_act = jnp.dot(flattened, gate_weight[0], preferred_element_type=f32)
    up_act = jnp.dot(flattened, up_weight[0], preferred_element_type=f32)
    hidden = (jax.nn.silu(gate_act) * up_act).astype(bf16)
    piece_out = jnp.dot(hidden, down_projection_weight[0], preferred_element_type=f32).astype(bf16)
    returned_rows = lax.all_to_all(
        piece_out.reshape(sources, item_count, feature_count),
        "expert",
        split_axis=0,
        concat_axis=0,
        tiled=True,
    )
    combiner = jnp.sum(
        route_weights[:, :, None]
        * (slot_ids[:, :, None] == slot_range[None, None, :]).astype(f32),
        axis=1,
    )
    summed = jnp.sum(
        returned_rows.reshape(experts, SHARDS, capacity, model_width).astype(f32), axis=1
    ).reshape(slot_count, model_width)
    expert_sum = jnp.dot(combiner, summed, precision=lax.Precision.HIGHEST)
    return (res32 + expert_sum).astype(bf16)


def solution(mesh):
    placed = (
        P(("group", "expert"), None),
        P(("group", "expert"), None, None),
        P(("group", "expert"), None),
        P(("group", "expert"), None, None),
        P(("group", "expert"), None, None),
        P(("group", "expert")),
        P("expert", None, None),
        P("expert", None),
        P(),
        P(("group", "expert"), None),
        P(("group", "expert"), None),
        P("expert", None, None),
        P("expert", None, None),
        P("expert", None, None),
    )
    return jax.shard_map(
        shards, mesh=mesh, in_specs=placed, out_specs=P(("group", "expert"), None), check_vma=False
    )
```

```python
import jax
import jax.numpy as jnp
from jax import lax
from jax.sharding import PartitionSpec as P

SHARDS = 8
LANES = 128
TILE = 128


score_scale = 192.0 ** (-0.5)
epsilon = 1e-06
route_scale = 2.5
f32 = jnp.float32
bf16 = jnp.bfloat16


def slot_table(routes, experts, capacity):
    flattened = routes.reshape(-1)
    onehot = (flattened[:, None] == jnp.arange(experts, dtype=jnp.int32)[None, :]).astype(jnp.int32)
    before = jnp.cumsum(onehot, axis=0) - onehot
    ranking = jnp.sum(before * onehot, axis=1)
    return (flattened * capacity + ranking).reshape(routes.shape)


def stage_bits(nbits):
    low = list(range(nbits))
    high = [0, 2, 1, *low[3:]]
    return list(zip(low, high, strict=True))


def chain_plans(nbits, width):
    stages = stage_bits(nbits)
    tiles = width // TILE
    plans, start = [], 0
    for order, share in (((1, 2, 3), 19), ((1, 2, 3), 19), ((1, 2, 3), 18)):
        order = [*order, *range(4, nbits - 1)]
        size = tiles * share // 56 * TILE
        plans.append((start, size, order, [stages[0], *[stages[k] for k in order], stages[-1]]))
        start += size
    return plans


def reorder(rows, old, new):
    shape = rows.shape
    axes = [*[old.index(k) for k in new], len(old), len(old) + 1]
    return rows.reshape(*(2,) * len(old), -1, shape[1]).transpose(axes).reshape(shape)


def swap(x, stage, devices):
    pairs = [(i, i ^ (1 << stage[i & 1])) for i in range(devices)]
    return lax.ppermute(x, "expert", pairs)


def row_sources(me, stages, devices, tokens_here):
    at = jnp.arange(devices * tokens_here, dtype=jnp.int32)
    place = at // tokens_here
    top = len(stages) - 1
    other = place >> top
    core = (me & 1) ^ other
    owner = me ^ other
    for step in range(1, len(stages)):
        bit = (place >> (top - step)) & 1
        owner = owner ^ jnp.where(core == 0, bit << stages[step][0], bit << stages[step][1])
    return owner * tokens_here + at % tokens_here


def add32(a, b):
    return a.astype(f32) + b.astype(f32)


def halve(keep, send, stages, devices):
    for step, stage in enumerate(stages[:-1]):
        came = swap(send, stage, devices)
        half = keep.shape[0] // 2
        send = add32(keep[half:], came[half:]).astype(bf16)
        keep = add32(keep[:half], came[:half])
        if step + 2 < len(stages):
            keep = keep.astype(bf16)
    return keep, send


def double(rows, stages, devices):
    for stage in stages[:0:-1]:
        rows = jnp.concatenate([rows, swap(rows, stage, devices)], axis=0)
    return rows, swap(rows, stages[0], devices)


def three_parts(x):
    parts = []
    for _ in range(3):
        part = lax.reduce_precision(x, 8, 7)
        parts.append(part.astype(bf16))
        x = x - part
    return parts


def attend(q_latent, q_rope, cache_latent, cache_rope, lengths):
    tokens_here, heads_all, _ = q_latent.shape
    rope_width = cache_rope.shape[1]
    cache_rows = cache_latent.shape[1]
    scores = jnp.einsum("thk,tlk->thl", q_latent, cache_latent, preferred_element_type=f32)
    scores = scores + jnp.einsum(
        "thr,trl->thl",
        q_rope.reshape(tokens_here, heads_all, rope_width),
        cache_rope,
        preferred_element_type=f32,
    )
    scores = scores * score_scale
    usable = jnp.arange(cache_rows, dtype=jnp.int32)[None, :] < lengths[:, None]
    scores = jnp.where(usable[:, None, :], scores, -jnp.inf)
    highest = jnp.max(scores, axis=2, keepdims=True)
    expd = jnp.exp(scores - highest)
    weights = (expd / jnp.sum(expd, axis=2, keepdims=True)).astype(bf16)
    return jnp.einsum("thl,tlk->thk", weights, cache_latent, preferred_element_type=f32).astype(bf16)


def shards(
    hidden_in,
    q_latent,
    q_rope,
    cache_latent,
    cache_rope,
    lengths,
    value_up_weight,
    out_weight,
    norm_gain,
    route_ids,
    route_logits,
    gate_weight,
    up_weight,
    down_projection_weight,
):
    devices = lax.axis_size("expert")
    me = lax.axis_index("expert")
    nbits = devices.bit_length() - 1
    tokens_here = hidden_in.shape[0]
    model_width = hidden_in.shape[1]
    top_count = route_ids.shape[1]
    experts = devices // SHARDS
    plans = chain_plans(nbits, model_width)
    base_order = plans[0][2]
    sigm = jax.nn.sigmoid(route_logits)
    route_weights = route_scale * sigm / jnp.sum(sigm, axis=1, keepdims=True)

    latent_out = attend(q_latent, q_rope, cache_latent, cache_rope, lengths)
    by_head = lax.all_to_all(latent_out, "expert", split_axis=1, concat_axis=0, tiled=True)
    head_values = jnp.einsum(
        "aqg,qge->aqe", by_head, value_up_weight, preferred_element_type=f32
    ).astype(bf16)
    rows = devices * tokens_here
    half = rows // 2
    head_values = head_values.reshape(rows, -1)
    chosen = route_ids[:, :, None] == jnp.arange(experts, dtype=jnp.int32)[None, None, :]
    shares = jnp.sum(jnp.where(chosen, route_weights[:, :, None], 0.0), axis=1)
    extra = jnp.concatenate(three_parts(shares), axis=1)
    extra = jnp.pad(extra, ((0, 0), (0, LANES - extra.shape[1])))
    dense = experts <= top_count

    residual = []
    for i, (start, size, _, stages) in enumerate(plans):
        source = row_sources(me, stages, devices, tokens_here)
        shuffle = (source[:, None] == jnp.arange(rows, dtype=jnp.int32)[None, :]).astype(bf16)
        values = jnp.dot(shuffle, head_values, preferred_element_type=f32).astype(bf16)
        weight = out_weight[:, start : start + size]
        send = jnp.dot(values[half:], weight, preferred_element_type=f32).astype(bf16)
        keep = jnp.dot(values[:half], weight, preferred_element_type=f32)
        own, partners = halve(keep, send, stages, devices)
        own = (own + hidden_in[:, start : start + size].astype(f32)).astype(bf16)
        both = jnp.concatenate([own, partners], axis=0)
        if dense and i + 1 == len(plans):
            beside = jnp.concatenate([extra, jnp.zeros_like(extra)], axis=0)
            both = jnp.concatenate([both, beside], axis=1)
        came = swap(both, stages[-1], devices)
        came = jnp.concatenate([came[tokens_here:], came[:tokens_here]], axis=0)
        residual.append(add32(both, came).astype(bf16))

    if not dense:
        return routed(
            jnp.concatenate(residual, axis=1)[:tokens_here],
            norm_gain,
            route_ids,
            route_weights,
            gate_weight,
            up_weight,
            down_projection_weight,
        )

    gate_act, up_act, squares = [0.0, 0.0], [0.0, 0.0], [0.0, 0.0]
    got = [None, None]
    for i, (start, size, order, stages) in enumerate(plans):
        gain = norm_gain[start : start + size].astype(f32)
        for h, taken in enumerate(double(residual[i], stages[:-1], devices)):
            if i + 1 == len(plans):
                got[h] = reorder(taken[:, size:].astype(f32), order, base_order)
                taken = taken[:, :size]
            wide = taken.astype(f32)
            parts = (
                jnp.sum(wide * wide, axis=1, keepdims=True),
                jnp.dot(
                    (wide * gain).astype(bf16),
                    gate_weight[0, start : start + size],
                    preferred_element_type=f32,
                ),
                jnp.dot(
                    (wide * gain).astype(bf16),
                    up_weight[0, start : start + size],
                    preferred_element_type=f32,
                ),
            )
            if order != base_order:
                parts = tuple(reorder(p, order, base_order) for p in parts)
            squares[h], gate_act[h], up_act[h] = (
                squares[h] + parts[0],
                gate_act[h] + parts[1],
                up_act[h] + parts[2],
            )
    lane = jnp.arange(LANES, dtype=jnp.int32)
    own = (lane % experts == me // SHARDS) & (lane < 3 * experts)
    hidden = []
    for h in range(2):
        factor = lax.rsqrt(squares[h] / model_width + epsilon)
        share = jnp.sum(jnp.where(own[None, :], got[h], 0.0), axis=1, keepdims=True)
        hidden.append(
            (jax.nn.silu(gate_act[h] * factor) * (up_act[h] * factor) * share).astype(bf16)
        )
    out = []
    for (start, size, order, stages), base in zip(plans, residual, strict=True):
        weight = down_projection_weight[0, :, start : start + size]
        acts = [reorder(x, base_order, order) for x in hidden] if order != base_order else hidden
        send = jnp.dot(acts[1], weight, preferred_element_type=f32).astype(bf16)
        keep = jnp.dot(acts[0], weight, preferred_element_type=f32)
        own, partners = halve(keep, send, stages, devices)
        came = swap(partners, stages[-1], devices)
        total = base[:tokens_here, :size].astype(f32) + own + came.astype(f32)
        out.append(total.astype(bf16))
    return jnp.concatenate(out, axis=1)


def routed(
    residual, norm_gain, route_ids, route_weights, gate_weight, up_weight, down_projection_weight
):
    devices = lax.axis_size("expert")
    tokens_here, model_width = residual.shape
    top_count = route_ids.shape[1]
    experts = devices // SHARDS
    capacity = min(tokens_here, max(2, (tokens_here * top_count + experts - 1) // experts + 1))
    slot_count = experts * capacity
    slot_ids = slot_table(route_ids, experts, capacity)
    slot_range = jnp.arange(slot_count, dtype=jnp.int32)
    res32 = residual.astype(f32)
    normed = (
        res32
        * lax.rsqrt(jnp.mean(res32 * res32, axis=1, keepdims=True) + epsilon)
        * norm_gain.astype(f32)
    ).astype(bf16)
    placement = jnp.sum(
        (slot_ids[:, :, None] == slot_range[None, None, :]).astype(jnp.int32), axis=1
    ).astype(bf16)
    outgoing = jnp.einsum("tq,tw->qw", placement, normed, preferred_element_type=f32).astype(bf16)
    outgoing = jnp.broadcast_to(
        outgoing.reshape(experts, 1, capacity, model_width),
        (experts, SHARDS, capacity, model_width),
    )
    outgoing = outgoing.reshape(devices, capacity, model_width)
    received = lax.all_to_all(outgoing, "expert", split_axis=0, concat_axis=0, tiled=True)
    sources, item_count, feature_count = received.shape
    flattened = received.reshape(sources * item_count, feature_count)
    gate_act = jnp.dot(flattened, gate_weight[0], preferred_element_type=f32)
    up_act = jnp.dot(flattened, up_weight[0], preferred_element_type=f32)
    hidden = (jax.nn.silu(gate_act) * up_act).astype(bf16)
    piece_out = jnp.dot(hidden, down_projection_weight[0], preferred_element_type=f32).astype(bf16)
    returned_rows = lax.all_to_all(
        piece_out.reshape(sources, item_count, feature_count),
        "expert",
        split_axis=0,
        concat_axis=0,
        tiled=True,
    )
    combiner = jnp.sum(
        route_weights[:, :, None]
        * (slot_ids[:, :, None] == slot_range[None, None, :]).astype(f32),
        axis=1,
    )
    summed = jnp.sum(
        returned_rows.reshape(experts, SHARDS, capacity, model_width).astype(f32), axis=1
    ).reshape(slot_count, model_width)
    expert_sum = jnp.dot(combiner, summed, precision=lax.Precision.HIGHEST)
    return (res32 + expert_sum).astype(bf16)


def solution(mesh):
    placed = (
        P(("group", "expert"), None),
        P(("group", "expert"), None, None),
        P(("group", "expert"), None),
        P(("group", "expert"), None, None),
        P(("group", "expert"), None, None),
        P(("group", "expert")),
        P("expert", None, None),
        P("expert", None),
        P(),
        P(("group", "expert"), None),
        P(("group", "expert"), None),
        P("expert", None, None),
        P("expert", None, None),
        P("expert", None, None),
    )
    return jax.shard_map(
        shards, mesh=mesh, in_specs=placed, out_specs=P(("group", "expert"), None), check_vma=False
    )
```

```python
import functools

import jax
import jax.numpy as jnp
import numpy as np
from jax import lax
from jax.experimental import pallas as pl
from jax.experimental.pallas import tpu as pltpu
from jax.sharding import PartitionSpec as P

SHARDS = 8
LANES = 128
TILE = 128
CHAINS = 3
COLUMNS = 640
ATTEND_VMEM = 56 << 20
PROJECT_VMEM = 32 << 20
FETCH_VMEM = 56 << 20


score_scale = 192.0 ** (-0.5)
epsilon = 1e-06
route_scale = 2.5
f32 = jnp.float32
bf16 = jnp.bfloat16


def slot_table(routes, experts, capacity):
    flattened = routes.reshape(-1)
    onehot = (flattened[:, None] == jnp.arange(experts, dtype=jnp.int32)[None, :]).astype(jnp.int32)
    before = jnp.cumsum(onehot, axis=0) - onehot
    ranking = jnp.sum(before * onehot, axis=1)
    return (flattened * capacity + ranking).reshape(routes.shape)


def stage_bits(nbits):
    low = list(range(nbits))
    high = [0, 2, 1, *low[3:]]
    return list(zip(low, high, strict=True))


def chain_parts(width):
    tiles = width // TILE
    sizes = [(tiles + i) // CHAINS * TILE for i in range(CHAINS)][::-1]
    return [(sum(sizes[:i]), size) for i, size in enumerate(sizes)]


def chain_orders(nbits):
    plain = list(range(1, nbits - 1))
    return [plain] * (CHAINS - 1) + [[3, 1, 2, *plain[3:]]]


def place_rows(order, rows):
    index = np.arange(rows).reshape(*(2,) * (len(order) + 1), -1)
    return index.transpose(0, *order, len(order) + 1).reshape(-1)


def swap(x, stage, devices):
    pairs = [(i, i ^ (1 << stage[i & 1])) for i in range(devices)]
    return lax.ppermute(x, "expert", pairs)


def row_sources(me, stages, devices, tokens_here):
    at = jnp.arange(devices * tokens_here, dtype=jnp.int32)
    place = at // tokens_here
    top = len(stages) - 1
    other = place >> top
    core = (me & 1) ^ other
    owner = me ^ other
    for step in range(1, len(stages)):
        bit = (place >> (top - step)) & 1
        owner = owner ^ jnp.where(core == 0, bit << stages[step][0], bit << stages[step][1])
    return owner * tokens_here + at % tokens_here


def add32(a, b):
    return a.astype(f32) + b.astype(f32)


def halve(keep, send, stages, devices):
    for step, stage in enumerate(stages[:-1]):
        came = swap(send, stage, devices)
        half = keep.shape[0] // 2
        send = add32(keep[half:], came[half:]).astype(bf16)
        keep = add32(keep[:half], came[:half])
        if step + 2 < len(stages):
            keep = keep.astype(bf16)
    return keep, send


def double(rows, stages, devices):
    for stage in stages[:0:-1]:
        rows = jnp.concatenate([rows, swap(rows, stage, devices)], axis=0)
    return rows, swap(rows, stages[0], devices)


def three_parts(x):
    parts = []
    for _ in range(3):
        part = lax.reduce_precision(x, 8, 7)
        parts.append(part.astype(bf16))
        x = x - part
    return parts


def attend_kernel(lengths_ref, latent_ref, rope_ref, keys_ref, turned_ref, out_ref, held_ref):
    token = pl.program_id(0)
    keys = keys_ref[0]
    scores = lax.dot_general(
        latent_ref[0], keys, (((1,), (1,)), ((), ())), preferred_element_type=f32
    )
    scores = scores + jnp.dot(rope_ref[0], turned_ref[0], preferred_element_type=f32)
    scores = scores * score_scale
    column = lax.broadcasted_iota(jnp.int32, scores.shape, 1)
    scores = jnp.where(column < lengths_ref[token], scores, -jnp.inf)
    expd = jnp.exp(scores - jnp.max(scores, axis=1, keepdims=True))
    weights = (expd / jnp.sum(expd, axis=1, keepdims=True)).astype(bf16)
    held_ref[token] = jnp.dot(weights, keys, preferred_element_type=f32)

    @pl.when(token == pl.num_programs(0) - 1)
    def _():
        out_ref[...] = jnp.swapaxes(held_ref[...], 0, 1).astype(bf16)


def attend(q_latent, q_rope, cache_latent, cache_rope, lengths):
    tokens, heads, rank = q_latent.shape
    _, turned, cached = cache_rope.shape
    at = lambda i: (i, 0, 0)
    return pl.pallas_call(
        attend_kernel,
        grid=(tokens,),
        out_shape=jax.ShapeDtypeStruct((heads, tokens, rank), bf16),
        in_specs=[
            pl.BlockSpec(memory_space=pltpu.SMEM),
            pl.BlockSpec((1, heads, rank), at),
            pl.BlockSpec((1, heads, turned), at),
            pl.BlockSpec((1, cached, rank), at),
            pl.BlockSpec((1, turned, cached), at),
        ],
        out_specs=pl.BlockSpec((heads, tokens, rank), lambda i: (0, 0, 0)),
        scratch_shapes=[pltpu.VMEM((tokens, heads, rank), f32)],
        compiler_params=pltpu.CompilerParams(vmem_limit_bytes=ATTEND_VMEM),
        cost_estimate=pl.CostEstimate(
            flops=2 * tokens * heads * cached * (2 * rank + turned),
            bytes_accessed=2 * tokens * (2 * heads * rank + cached * (rank + turned)),
            transcendentals=tokens * heads * cached,
        ),
    )(lengths, q_latent, q_rope.reshape(tokens, heads, turned), cache_latent, cache_rope)


def fetch_kernel(after_ref, gate_ref, up_ref, down_ref, both_held, down_held, done):
    width = gate_ref.shape[2]
    copies = [
        pltpu.make_async_copy(gate_ref.at[0], both_held.at[:, :width], done.at[0]),
        pltpu.make_async_copy(up_ref.at[0], both_held.at[:, width:], done.at[1]),
        pltpu.make_async_copy(down_ref.at[0], down_held, done.at[2]),
    ]
    for copy in copies:
        copy.start()
    for copy in copies:
        copy.wait()


def fetch(after, gate_weight, up_weight, down_projection_weight):
    _, model_width, width = gate_weight.shape
    shapes = [(model_width, 2 * width), (width, model_width)]
    size = sum(2 * a * b for a, b in shapes)
    return pl.pallas_call(
        fetch_kernel,
        out_shape=[jax.ShapeDtypeStruct(shape, bf16) for shape in shapes],
        in_specs=[pl.BlockSpec(memory_space=pl.ANY)] * 4,
        out_specs=[pl.BlockSpec(memory_space=pltpu.VMEM)] * 2,
        scratch_shapes=[pltpu.SemaphoreType.DMA((3,))],
        compiler_params=pltpu.CompilerParams(vmem_limit_bytes=FETCH_VMEM),
        cost_estimate=pl.CostEstimate(flops=0, bytes_accessed=2 * size, transcendentals=0),
    )(after, gate_weight, up_weight, down_projection_weight)


def project_kernel(start, values_ref, weight_ref, keep_ref, send_ref):
    half, size = keep_ref.shape
    for at in range(0, size, COLUMNS):
        width = min(COLUMNS, size - at)
        out = jnp.dot(
            values_ref[...],
            weight_ref[:, start + at : start + at + width],
            preferred_element_type=f32,
        ).astype(bf16)
        keep_ref[:, at : at + width] = out[:half]
        send_ref[:, at : at + width] = out[half:]


def project(values, weight, start, size):
    rows, depth = values.shape
    half = jax.ShapeDtypeStruct((rows // 2, size), bf16)
    return pl.pallas_call(
        functools.partial(project_kernel, start),
        out_shape=[half, half],
        in_specs=[pl.BlockSpec(memory_space=pltpu.VMEM)] * 2,
        out_specs=[pl.BlockSpec(memory_space=pltpu.VMEM)] * 2,
        compiler_params=pltpu.CompilerParams(vmem_limit_bytes=PROJECT_VMEM),
        cost_estimate=pl.CostEstimate(
            flops=2 * rows * depth * size,
            bytes_accessed=2 * (rows * depth + depth * size + rows * size),
            transcendentals=0,
        ),
    )(values, weight)


def shards(
    hidden_in,
    q_latent,
    q_rope,
    cache_latent,
    cache_rope,
    lengths,
    value_up_weight,
    out_weight,
    norm_gain,
    route_ids,
    route_logits,
    gate_weight,
    up_weight,
    down_projection_weight,
):
    devices = lax.axis_size("expert")
    me = lax.axis_index("expert")
    nbits = devices.bit_length() - 1
    tokens_here = hidden_in.shape[0]
    model_width = hidden_in.shape[1]
    top_count = route_ids.shape[1]
    experts = devices // SHARDS
    stages = stage_bits(nbits)
    plans = chain_parts(model_width)
    orders = chain_orders(nbits)
    sum_stages = [[stages[0], *[stages[k] for k in order], stages[-1]] for order in orders]
    sigm = jax.nn.sigmoid(route_logits)
    route_weights = route_scale * sigm / jnp.sum(sigm, axis=1, keepdims=True)

    latent_out = attend(q_latent, q_rope, cache_latent, cache_rope, lengths)
    both_near, down_near = fetch(latent_out, gate_weight, up_weight, down_projection_weight)
    _, out_after = lax.optimization_barrier((latent_out, out_weight))
    out_near = [out_after[:, start : start + size] for start, size in plans]
    value_up_weight, both_near, down_near, *out_near = lax.optimization_barrier(
        (value_up_weight, both_near, down_near, *out_near)
    )
    by_head = lax.all_to_all(latent_out, "expert", split_axis=0, concat_axis=0, tiled=True)
    heads_here = value_up_weight.shape[0]
    by_head = by_head.reshape(devices, heads_here, tokens_here, -1)
    head_values = jnp.einsum(
        "sqtg,qge->stqe", by_head, value_up_weight, preferred_element_type=f32
    ).astype(bf16)
    rows = devices * tokens_here
    head_values = head_values.reshape(rows, -1)
    at = jnp.arange(rows, dtype=jnp.int32)
    values = {}
    for order, its in zip(orders, sum_stages, strict=True):
        if tuple(order) not in values:
            source = row_sources(me, its, devices, tokens_here)
            shuffle = (source[:, None] == at[None, :]).astype(bf16)
            values[tuple(order)] = jnp.dot(
                shuffle, head_values, preferred_element_type=f32
            ).astype(bf16)

    chosen = route_ids[:, :, None] == jnp.arange(experts, dtype=jnp.int32)[None, None, :]
    shares = jnp.sum(jnp.where(chosen, route_weights[:, :, None], 0.0), axis=1)
    extra = jnp.concatenate(three_parts(shares), axis=1)
    extra = jnp.pad(extra, ((0, 0), (0, LANES - extra.shape[1])))
    dense = experts <= top_count

    residual = []
    for i, (start, size) in enumerate(plans):
        keep, send = project(values[tuple(orders[i])], out_near[i], 0, size)
        own, partners = halve(keep, send, sum_stages[i], devices)
        own = (own + hidden_in[:, start : start + size].astype(f32)).astype(bf16)
        both = jnp.concatenate([own, partners], axis=0)
        if dense and i + 1 == len(plans):
            beside = jnp.concatenate([extra, jnp.zeros_like(extra)], axis=0)
            both = jnp.concatenate([both, beside], axis=1)
        came = swap(both, stages[-1], devices)
        came = jnp.concatenate([came[tokens_here:], came[:tokens_here]], axis=0)
        residual.append(add32(both, came).astype(bf16))

    if not dense:
        return routed(
            jnp.concatenate(residual, axis=1)[:tokens_here],
            norm_gain,
            route_ids,
            route_weights,
            gate_weight,
            up_weight,
            down_projection_weight,
        )

    acts, squares, got = [0.0, 0.0], [0.0, 0.0], [None, None]
    for i, (start, size) in enumerate(plans):
        gain = norm_gain[start : start + size].astype(f32)
        for h, taken in enumerate(double(residual[i], stages[:-1], devices)):
            if i + 1 == len(plans):
                got[h] = taken[:, size:].astype(f32)
                taken = taken[:, :size]
            wide = taken.astype(f32)
            squares[h] = squares[h] + jnp.sum(wide * wide, axis=1, keepdims=True)
            acts[h] = acts[h] + jnp.dot(
                (wide * gain).astype(bf16),
                both_near[start : start + size],
                preferred_element_type=f32,
            )
    lane = jnp.arange(LANES, dtype=jnp.int32)
    own = (lane % experts == me // SHARDS) & (lane < 3 * experts)
    hidden = []
    for h in range(2):
        factor = lax.rsqrt(squares[h] / model_width + epsilon)
        share = jnp.sum(jnp.where(own[None, :], got[h], 0.0), axis=1, keepdims=True)
        gate_act, up_act = jnp.split(acts[h] * factor, 2, axis=1)
        hidden.append((jax.nn.silu(gate_act) * up_act * share).astype(bf16))
    hidden = jnp.concatenate(hidden, axis=0)
    out = []
    for i, ((start, size), base) in enumerate(zip(plans, residual, strict=True)):
        acts = hidden
        if orders[i] != orders[0]:
            move = np.eye(rows, dtype=np.float32)[place_rows(orders[i], rows)]
            acts = jnp.dot(jnp.asarray(move, bf16), hidden, preferred_element_type=f32).astype(bf16)
        keep, send = project(acts, down_near, start, size)
        own, partners = halve(keep, send, sum_stages[i], devices)
        came = swap(partners, stages[-1], devices)
        total = base[:tokens_here, :size].astype(f32) + own + came.astype(f32)
        out.append(total.astype(bf16))
    return jnp.concatenate(out, axis=1)


def routed(
    residual, norm_gain, route_ids, route_weights, gate_weight, up_weight, down_projection_weight
):
    devices = lax.axis_size("expert")
    tokens_here, model_width = residual.shape
    top_count = route_ids.shape[1]
    experts = devices // SHARDS
    capacity = min(tokens_here, max(2, (tokens_here * top_count + experts - 1) // experts + 1))
    slot_count = experts * capacity
    slot_ids = slot_table(route_ids, experts, capacity)
    slot_range = jnp.arange(slot_count, dtype=jnp.int32)
    res32 = residual.astype(f32)
    normed = (
        res32
        * lax.rsqrt(jnp.mean(res32 * res32, axis=1, keepdims=True) + epsilon)
        * norm_gain.astype(f32)
    ).astype(bf16)
    placement = jnp.sum(
        (slot_ids[:, :, None] == slot_range[None, None, :]).astype(jnp.int32), axis=1
    ).astype(bf16)
    outgoing = jnp.einsum("tq,tw->qw", placement, normed, preferred_element_type=f32).astype(bf16)
    outgoing = jnp.broadcast_to(
        outgoing.reshape(experts, 1, capacity, model_width),
        (experts, SHARDS, capacity, model_width),
    )
    outgoing = outgoing.reshape(devices, capacity, model_width)
    received = lax.all_to_all(outgoing, "expert", split_axis=0, concat_axis=0, tiled=True)
    sources, item_count, feature_count = received.shape
    flattened = received.reshape(sources * item_count, feature_count)
    gate_act = jnp.dot(flattened, gate_weight[0], preferred_element_type=f32)
    up_act = jnp.dot(flattened, up_weight[0], preferred_element_type=f32)
    hidden = (jax.nn.silu(gate_act) * up_act).astype(bf16)
    piece_out = jnp.dot(hidden, down_projection_weight[0], preferred_element_type=f32).astype(bf16)
    returned_rows = lax.all_to_all(
        piece_out.reshape(sources, item_count, feature_count),
        "expert",
        split_axis=0,
        concat_axis=0,
        tiled=True,
    )
    combiner = jnp.sum(
        route_weights[:, :, None]
        * (slot_ids[:, :, None] == slot_range[None, None, :]).astype(f32),
        axis=1,
    )
    summed = jnp.sum(
        returned_rows.reshape(experts, SHARDS, capacity, model_width).astype(f32), axis=1
    ).reshape(slot_count, model_width)
    expert_sum = jnp.dot(combiner, summed, precision=lax.Precision.HIGHEST)
    return (res32 + expert_sum).astype(bf16)


def solution(mesh):
    placed = (
        P(("group", "expert"), None),
        P(("group", "expert"), None, None),
        P(("group", "expert"), None),
        P(("group", "expert"), None, None),
        P(("group", "expert"), None, None),
        P(("group", "expert")),
        P("expert", None, None),
        P("expert", None),
        P(),
        P(("group", "expert"), None),
        P(("group", "expert"), None),
        P("expert", None, None),
        P("expert", None, None),
        P("expert", None, None),
    )
    return jax.shard_map(
        shards, mesh=mesh, in_specs=placed, out_specs=P(("group", "expert"), None), check_vma=False
    )
```

```python
import functools

import jax
import jax.numpy as jnp
import numpy as np
from jax import lax
from jax.experimental import pallas as pl
from jax.experimental.pallas import tpu as pltpu
from jax.sharding import PartitionSpec as P

SHARDS = 8
LANES = 128
TILE = 128
CHAINS = 3
COLUMNS = 640
ATTEND_VMEM = 56 << 20
PROJECT_VMEM = 32 << 20
FETCH_VMEM = 56 << 20


score_scale = 192.0 ** (-0.5)
epsilon = 1e-06
route_scale = 2.5
f32 = jnp.float32
bf16 = jnp.bfloat16


def slot_table(routes, experts, capacity):
    flattened = routes.reshape(-1)
    onehot = (flattened[:, None] == jnp.arange(experts, dtype=jnp.int32)[None, :]).astype(jnp.int32)
    before = jnp.cumsum(onehot, axis=0) - onehot
    ranking = jnp.sum(before * onehot, axis=1)
    return (flattened * capacity + ranking).reshape(routes.shape)


def stage_bits(nbits):
    low = list(range(nbits))
    high = [0, 2, 1, *low[3:]]
    return list(zip(low, high, strict=True))


def chain_parts(width):
    tiles = width // TILE
    sizes = [(tiles + i) // CHAINS * TILE for i in range(CHAINS)][::-1]
    return [(sum(sizes[:i]), size) for i, size in enumerate(sizes)]


def chain_orders(nbits):
    plain = list(range(1, nbits - 1))
    return [[3, 1, 2, *plain[3:]]] + [plain] * (CHAINS - 1)


def place_rows(order, rows):
    index = np.arange(rows).reshape(*(2,) * (len(order) + 1), -1)
    return index.transpose(0, *order, len(order) + 1).reshape(-1)


def swap(x, stage, devices):
    pairs = [(i, i ^ (1 << stage[i & 1])) for i in range(devices)]
    return lax.ppermute(x, "expert", pairs)


def row_sources(me, stages, devices, tokens_here):
    at = jnp.arange(devices * tokens_here, dtype=jnp.int32)
    place = at // tokens_here
    top = len(stages) - 1
    other = place >> top
    core = (me & 1) ^ other
    owner = me ^ other
    for step in range(1, len(stages)):
        bit = (place >> (top - step)) & 1
        owner = owner ^ jnp.where(core == 0, bit << stages[step][0], bit << stages[step][1])
    return owner * tokens_here + at % tokens_here


def add32(a, b):
    return a.astype(f32) + b.astype(f32)


def halve(keep, send, stages, devices):
    for step, stage in enumerate(stages[:-1]):
        came = swap(send, stage, devices)
        half = keep.shape[0] // 2
        send = add32(keep[half:], came[half:]).astype(bf16)
        keep = add32(keep[:half], came[:half])
        if step + 2 < len(stages):
            keep = keep.astype(bf16)
    return keep, send


def double(rows, stages, devices):
    for stage in stages[:0:-1]:
        rows = jnp.concatenate([rows, swap(rows, stage, devices)], axis=0)
    return rows, swap(rows, stages[0], devices)


def three_parts(x):
    parts = []
    for _ in range(3):
        part = lax.reduce_precision(x, 8, 7)
        parts.append(part.astype(bf16))
        x = x - part
    return parts


def attend_kernel(lengths_ref, latent_ref, rope_ref, keys_ref, turned_ref, out_ref, held_ref):
    step = pl.program_id(0)
    group = keys_ref.shape[0]
    for i in range(group):
        token = step * group + i
        keys = keys_ref[i]
        scores = lax.dot_general(
            latent_ref[i], keys, (((1,), (1,)), ((), ())), preferred_element_type=f32
        )
        scores = scores + jnp.dot(rope_ref[i], turned_ref[i], preferred_element_type=f32)
        scores = scores * score_scale
        column = lax.broadcasted_iota(jnp.int32, scores.shape, 1)
        scores = jnp.where(column < lengths_ref[token], scores, -jnp.inf)
        expd = jnp.exp(scores - jnp.max(scores, axis=1, keepdims=True))
        weights = (expd * (1.0 / jnp.sum(expd, axis=1, keepdims=True))).astype(bf16)
        held_ref[token] = jnp.dot(weights, keys, preferred_element_type=f32)

    @pl.when(step == pl.num_programs(0) - 1)
    def _():
        out_ref[...] = jnp.swapaxes(held_ref[...], 0, 1).astype(bf16)


def attend(q_latent, q_rope, cache_latent, cache_rope, lengths):
    tokens, heads, rank = q_latent.shape
    _, turned, cached = cache_rope.shape
    at = lambda i: (i, 0, 0)
    group = 2 if tokens % 2 == 0 else 1
    return pl.pallas_call(
        attend_kernel,
        grid=(tokens // group,),
        out_shape=jax.ShapeDtypeStruct((heads, tokens, rank), bf16),
        in_specs=[
            pl.BlockSpec(memory_space=pltpu.SMEM),
            pl.BlockSpec((group, heads, rank), at),
            pl.BlockSpec((group, heads, turned), at),
            pl.BlockSpec((group, cached, rank), at),
            pl.BlockSpec((group, turned, cached), at),
        ],
        out_specs=pl.BlockSpec((heads, tokens, rank), lambda i: (0, 0, 0)),
        scratch_shapes=[pltpu.VMEM((tokens, heads, rank), f32)],
        compiler_params=pltpu.CompilerParams(vmem_limit_bytes=ATTEND_VMEM),
        cost_estimate=pl.CostEstimate(
            flops=2 * tokens * heads * cached * (2 * rank + turned),
            bytes_accessed=2 * tokens * (2 * heads * rank + cached * (rank + turned)),
            transcendentals=tokens * heads * cached,
        ),
    )(lengths, q_latent, q_rope.reshape(tokens, heads, turned), cache_latent, cache_rope)


def fetch_kernel(after_ref, gate_ref, up_ref, down_ref, both_held, down_held, done):
    width = gate_ref.shape[2]
    copies = [
        pltpu.make_async_copy(gate_ref.at[0], both_held.at[:, :width], done.at[0]),
        pltpu.make_async_copy(up_ref.at[0], both_held.at[:, width:], done.at[1]),
        pltpu.make_async_copy(down_ref.at[0], down_held, done.at[2]),
    ]
    for copy in copies:
        copy.start()
    for copy in copies:
        copy.wait()


def fetch(after, gate_weight, up_weight, down_projection_weight):
    _, model_width, width = gate_weight.shape
    shapes = [(model_width, 2 * width), (width, model_width)]
    size = sum(2 * a * b for a, b in shapes)
    return pl.pallas_call(
        fetch_kernel,
        out_shape=[jax.ShapeDtypeStruct(shape, bf16) for shape in shapes],
        in_specs=[pl.BlockSpec(memory_space=pl.ANY)] * 4,
        out_specs=[pl.BlockSpec(memory_space=pltpu.VMEM)] * 2,
        scratch_shapes=[pltpu.SemaphoreType.DMA((3,))],
        compiler_params=pltpu.CompilerParams(vmem_limit_bytes=FETCH_VMEM),
        cost_estimate=pl.CostEstimate(flops=0, bytes_accessed=2 * size, transcendentals=0),
    )(after, gate_weight, up_weight, down_projection_weight)


def project_kernel(start, values_ref, weight_ref, keep_ref, send_ref):
    half, size = keep_ref.shape
    for at in range(0, size, COLUMNS):
        width = min(COLUMNS, size - at)
        out = jnp.dot(
            values_ref[...],
            weight_ref[:, start + at : start + at + width],
            preferred_element_type=f32,
        ).astype(bf16)
        keep_ref[:, at : at + width] = out[:half]
        send_ref[:, at : at + width] = out[half:]


def project(values, weight, start, size):
    rows, depth = values.shape
    half = jax.ShapeDtypeStruct((rows // 2, size), bf16)
    return pl.pallas_call(
        functools.partial(project_kernel, start),
        out_shape=[half, half],
        in_specs=[pl.BlockSpec(memory_space=pltpu.VMEM)] * 2,
        out_specs=[pl.BlockSpec(memory_space=pltpu.VMEM)] * 2,
        compiler_params=pltpu.CompilerParams(vmem_limit_bytes=PROJECT_VMEM),
        cost_estimate=pl.CostEstimate(
            flops=2 * rows * depth * size,
            bytes_accessed=2 * (rows * depth + depth * size + rows * size),
            transcendentals=0,
        ),
    )(values, weight)


def shards(
    hidden_in,
    q_latent,
    q_rope,
    cache_latent,
    cache_rope,
    lengths,
    value_up_weight,
    out_weight,
    norm_gain,
    route_ids,
    route_logits,
    gate_weight,
    up_weight,
    down_projection_weight,
):
    devices = lax.axis_size("expert")
    me = lax.axis_index("expert")
    nbits = devices.bit_length() - 1
    tokens_here = hidden_in.shape[0]
    model_width = hidden_in.shape[1]
    top_count = route_ids.shape[1]
    experts = devices // SHARDS
    stages = stage_bits(nbits)
    plans = chain_parts(model_width)
    orders = chain_orders(nbits)
    sum_stages = [[stages[0], *[stages[k] for k in order], stages[-1]] for order in orders]
    sigm = jax.nn.sigmoid(route_logits)
    route_weights = route_scale * sigm / jnp.sum(sigm, axis=1, keepdims=True)

    latent_out = attend(q_latent, q_rope, cache_latent, cache_rope, lengths)
    both_near, down_near = fetch(latent_out, gate_weight, up_weight, down_projection_weight)
    _, out_after = lax.optimization_barrier((latent_out, out_weight))
    out_near = [out_after[:, start : start + size] for start, size in plans]
    value_up_weight, both_near, down_near, *out_near = lax.optimization_barrier(
        (value_up_weight, both_near, down_near, *out_near)
    )
    by_head = lax.all_to_all(latent_out, "expert", split_axis=0, concat_axis=0, tiled=True)
    heads_here = value_up_weight.shape[0]
    by_head = by_head.reshape(devices, heads_here, tokens_here, -1)
    head_values = jnp.einsum(
        "sqtg,qge->stqe", by_head, value_up_weight, preferred_element_type=f32
    ).astype(bf16)
    rows = devices * tokens_here
    head_values = head_values.reshape(rows, -1)
    at = jnp.arange(rows, dtype=jnp.int32)
    values = {}
    for order, its in zip(orders, sum_stages, strict=True):
        if tuple(order) not in values:
            source = row_sources(me, its, devices, tokens_here)
            shuffle = (source[:, None] == at[None, :]).astype(bf16)
            values[tuple(order)] = jnp.dot(
                shuffle, head_values, preferred_element_type=f32
            ).astype(bf16)

    chosen = route_ids[:, :, None] == jnp.arange(experts, dtype=jnp.int32)[None, None, :]
    shares = jnp.sum(jnp.where(chosen, route_weights[:, :, None], 0.0), axis=1)
    extra = jnp.concatenate(three_parts(shares), axis=1)
    extra = jnp.pad(extra, ((0, 0), (0, LANES - extra.shape[1])))
    dense = experts <= top_count

    residual = []
    for i, (start, size) in enumerate(plans):
        keep, send = project(values[tuple(orders[i])], out_near[i], 0, size)
        own, partners = halve(keep, send, sum_stages[i], devices)
        own = (own + hidden_in[:, start : start + size].astype(f32)).astype(bf16)
        both = jnp.concatenate([own, partners], axis=0)
        if dense and i + 1 == len(plans):
            beside = jnp.concatenate([extra, jnp.zeros_like(extra)], axis=0)
            both = jnp.concatenate([both, beside], axis=1)
        came = swap(both, stages[-1], devices)
        came = jnp.concatenate([came[tokens_here:], came[:tokens_here]], axis=0)
        residual.append(add32(both, came).astype(bf16))

    if not dense:
        return routed(
            jnp.concatenate(residual, axis=1)[:tokens_here],
            norm_gain,
            route_ids,
            route_weights,
            gate_weight,
            up_weight,
            down_projection_weight,
        )

    acts, squares, got = [0.0, 0.0], [0.0, 0.0], [None, None]
    for i, (start, size) in enumerate(plans):
        gain = norm_gain[start : start + size].astype(f32)
        for h, taken in enumerate(double(residual[i], stages[:-1], devices)):
            if i + 1 == len(plans):
                got[h] = taken[:, size:].astype(f32)
                taken = taken[:, :size]
            wide = taken.astype(f32)
            squares[h] = squares[h] + jnp.sum(wide * wide, axis=1, keepdims=True)
            acts[h] = acts[h] + jnp.dot(
                (wide * gain).astype(bf16),
                both_near[start : start + size],
                preferred_element_type=f32,
            )
    lane = jnp.arange(LANES, dtype=jnp.int32)
    own = (lane % experts == me // SHARDS) & (lane < 3 * experts)
    hidden = []
    for h in range(2):
        factor = lax.rsqrt(squares[h] / model_width + epsilon)
        share = jnp.sum(jnp.where(own[None, :], got[h], 0.0), axis=1, keepdims=True)
        gate_act, up_act = jnp.split(acts[h] * factor, 2, axis=1)
        hidden.append((jax.nn.silu(gate_act) * up_act * share).astype(bf16))
    hidden = jnp.concatenate(hidden, axis=0)
    out = []
    for i, ((start, size), base) in enumerate(zip(plans, residual, strict=True)):
        acts = hidden
        if orders[i] != sorted(orders[i]):
            move = np.eye(rows, dtype=np.float32)[place_rows(orders[i], rows)]
            acts = jnp.dot(jnp.asarray(move, bf16), hidden, preferred_element_type=f32).astype(bf16)
        keep, send = project(acts, down_near, start, size)
        own, partners = halve(keep, send, sum_stages[i], devices)
        came = swap(partners, stages[-1], devices)
        total = base[:tokens_here, :size].astype(f32) + own + came.astype(f32)
        out.append(total.astype(bf16))
    return jnp.concatenate(out, axis=1)


def routed(
    residual, norm_gain, route_ids, route_weights, gate_weight, up_weight, down_projection_weight
):
    devices = lax.axis_size("expert")
    tokens_here, model_width = residual.shape
    top_count = route_ids.shape[1]
    experts = devices // SHARDS
    capacity = min(tokens_here, max(2, (tokens_here * top_count + experts - 1) // experts + 1))
    slot_count = experts * capacity
    slot_ids = slot_table(route_ids, experts, capacity)
    slot_range = jnp.arange(slot_count, dtype=jnp.int32)
    res32 = residual.astype(f32)
    normed = (
        res32
        * lax.rsqrt(jnp.mean(res32 * res32, axis=1, keepdims=True) + epsilon)
        * norm_gain.astype(f32)
    ).astype(bf16)
    placement = jnp.sum(
        (slot_ids[:, :, None] == slot_range[None, None, :]).astype(jnp.int32), axis=1
    ).astype(bf16)
    outgoing = jnp.einsum("tq,tw->qw", placement, normed, preferred_element_type=f32).astype(bf16)
    outgoing = jnp.broadcast_to(
        outgoing.reshape(experts, 1, capacity, model_width),
        (experts, SHARDS, capacity, model_width),
    )
    outgoing = outgoing.reshape(devices, capacity, model_width)
    received = lax.all_to_all(outgoing, "expert", split_axis=0, concat_axis=0, tiled=True)
    sources, item_count, feature_count = received.shape
    flattened = received.reshape(sources * item_count, feature_count)
    gate_act = jnp.dot(flattened, gate_weight[0], preferred_element_type=f32)
    up_act = jnp.dot(flattened, up_weight[0], preferred_element_type=f32)
    hidden = (jax.nn.silu(gate_act) * up_act).astype(bf16)
    piece_out = jnp.dot(hidden, down_projection_weight[0], preferred_element_type=f32).astype(bf16)
    returned_rows = lax.all_to_all(
        piece_out.reshape(sources, item_count, feature_count),
        "expert",
        split_axis=0,
        concat_axis=0,
        tiled=True,
    )
    combiner = jnp.sum(
        route_weights[:, :, None]
        * (slot_ids[:, :, None] == slot_range[None, None, :]).astype(f32),
        axis=1,
    )
    summed = jnp.sum(
        returned_rows.reshape(experts, SHARDS, capacity, model_width).astype(f32), axis=1
    ).reshape(slot_count, model_width)
    expert_sum = jnp.dot(combiner, summed, precision=lax.Precision.HIGHEST)
    return (res32 + expert_sum).astype(bf16)


def solution(mesh):
    placed = (
        P(("group", "expert"), None),
        P(("group", "expert"), None, None),
        P(("group", "expert"), None),
        P(("group", "expert"), None, None),
        P(("group", "expert"), None, None),
        P(("group", "expert")),
        P("expert", None, None),
        P("expert", None),
        P(),
        P(("group", "expert"), None),
        P(("group", "expert"), None),
        P("expert", None, None),
        P("expert", None, None),
        P("expert", None, None),
    )
    return jax.shard_map(
        shards, mesh=mesh, in_specs=placed, out_specs=P(("group", "expert"), None), check_vma=False
    )
```

```python
import functools

import jax
import jax.numpy as jnp
import numpy as np
from jax import lax
from jax.experimental import pallas as pl
from jax.experimental.pallas import tpu as pltpu
from jax.sharding import PartitionSpec as P

SHARDS = 8
LANES = 128
TILE = 128
CHAINS = 3
COLUMNS = 640
ATTEND_VMEM = 56 << 20
PROJECT_VMEM = 32 << 20


score_scale = 192.0 ** (-0.5)
epsilon = 1e-06
route_scale = 2.5
f32 = jnp.float32
bf16 = jnp.bfloat16


def slot_table(routes, experts, capacity):
    flattened = routes.reshape(-1)
    onehot = (flattened[:, None] == jnp.arange(experts, dtype=jnp.int32)[None, :]).astype(jnp.int32)
    before = jnp.cumsum(onehot, axis=0) - onehot
    ranking = jnp.sum(before * onehot, axis=1)
    return (flattened * capacity + ranking).reshape(routes.shape)


def stage_bits(nbits):
    low = list(range(nbits))
    high = [0, 2, 1, *low[3:]]
    return list(zip(low, high, strict=True))


def chain_parts(width):
    tiles = width // TILE
    sizes = [(tiles + i) // CHAINS * TILE for i in range(CHAINS)][::-1]
    return [(sum(sizes[:i]), size) for i, size in enumerate(sizes)]


def chain_orders(nbits):
    plain = list(range(1, nbits - 1))
    return [[3, 1, 2, *plain[3:]]] + [plain] * (CHAINS - 1)


def place_rows(order, rows):
    index = np.arange(rows).reshape(*(2,) * (len(order) + 1), -1)
    return index.transpose(0, *order, len(order) + 1).reshape(-1)


def swap(x, stage, devices):
    pairs = [(i, i ^ (1 << stage[i & 1])) for i in range(devices)]
    return lax.ppermute(x, "expert", pairs)


def row_sources(me, stages, devices, tokens_here):
    at = jnp.arange(devices * tokens_here, dtype=jnp.int32)
    place = at // tokens_here
    top = len(stages) - 1
    other = place >> top
    core = (me & 1) ^ other
    owner = me ^ other
    for step in range(1, len(stages)):
        bit = (place >> (top - step)) & 1
        owner = owner ^ jnp.where(core == 0, bit << stages[step][0], bit << stages[step][1])
    return owner * tokens_here + at % tokens_here


def add32(a, b):
    return a.astype(f32) + b.astype(f32)


def halve(keep, send, stages, devices):
    for step, stage in enumerate(stages[:-1]):
        came = swap(send, stage, devices)
        half = keep.shape[0] // 2
        send = add32(keep[half:], came[half:]).astype(bf16)
        keep = add32(keep[:half], came[:half])
        if step + 2 < len(stages):
            keep = keep.astype(bf16)
    return keep, send


def double(rows, stages, devices):
    for stage in stages[:0:-1]:
        rows = jnp.concatenate([rows, swap(rows, stage, devices)], axis=0)
    return rows, swap(rows, stages[0], devices)


def three_parts(x):
    parts = []
    for _ in range(3):
        part = lax.reduce_precision(x, 8, 7)
        parts.append(part.astype(bf16))
        x = x - part
    return parts


def attend_kernel(lengths_ref, latent_ref, rope_ref, keys_ref, turned_ref, out_ref, held_ref):
    step = pl.program_id(0)
    group = keys_ref.shape[0]
    for i in range(group):
        token = step * group + i
        keys = keys_ref[i]
        scores = lax.dot_general(
            latent_ref[i], keys, (((1,), (1,)), ((), ())), preferred_element_type=f32
        )
        scores = scores + jnp.dot(rope_ref[i], turned_ref[i], preferred_element_type=f32)
        scores = scores * score_scale
        column = lax.broadcasted_iota(jnp.int32, scores.shape, 1)
        scores = jnp.where(column < lengths_ref[token], scores, -jnp.inf)
        expd = jnp.exp(scores - jnp.max(scores, axis=1, keepdims=True))
        weights = (expd * (1.0 / jnp.sum(expd, axis=1, keepdims=True))).astype(bf16)
        held_ref[token] = jnp.dot(weights, keys, preferred_element_type=f32)

    @pl.when(step == pl.num_programs(0) - 1)
    def _():
        out_ref[...] = jnp.swapaxes(held_ref[...], 0, 1).astype(bf16)


def attend(q_latent, q_rope, cache_latent, cache_rope, lengths):
    tokens, heads, rank = q_latent.shape
    _, turned, cached = cache_rope.shape
    at = lambda i: (i, 0, 0)
    group = 2 if tokens % 2 == 0 else 1
    return pl.pallas_call(
        attend_kernel,
        grid=(tokens // group,),
        out_shape=jax.ShapeDtypeStruct((heads, tokens, rank), bf16),
        in_specs=[
            pl.BlockSpec(memory_space=pltpu.SMEM),
            pl.BlockSpec((group, heads, rank), at),
            pl.BlockSpec((group, heads, turned), at),
            pl.BlockSpec((group, cached, rank), at),
            pl.BlockSpec((group, turned, cached), at),
        ],
        out_specs=pl.BlockSpec((heads, tokens, rank), lambda i: (0, 0, 0)),
        scratch_shapes=[pltpu.VMEM((tokens, heads, rank), f32)],
        compiler_params=pltpu.CompilerParams(vmem_limit_bytes=ATTEND_VMEM),
        cost_estimate=pl.CostEstimate(
            flops=2 * tokens * heads * cached * (2 * rank + turned),
            bytes_accessed=2 * tokens * (2 * heads * rank + cached * (rank + turned)),
            transcendentals=tokens * heads * cached,
        ),
    )(lengths, q_latent, q_rope.reshape(tokens, heads, turned), cache_latent, cache_rope)


def project_kernel(start, values_ref, weight_ref, keep_ref, send_ref):
    half, size = keep_ref.shape
    for at in range(0, size, COLUMNS):
        width = min(COLUMNS, size - at)
        out = jnp.dot(
            values_ref[...],
            weight_ref[:, start + at : start + at + width],
            preferred_element_type=f32,
        ).astype(bf16)
        keep_ref[:, at : at + width] = out[:half]
        send_ref[:, at : at + width] = out[half:]


def project(values, weight, start, size):
    rows, depth = values.shape
    half = jax.ShapeDtypeStruct((rows // 2, size), bf16)
    return pl.pallas_call(
        functools.partial(project_kernel, start),
        out_shape=[half, half],
        in_specs=[pl.BlockSpec(memory_space=pltpu.VMEM)] * 2,
        out_specs=[pl.BlockSpec(memory_space=pltpu.VMEM)] * 2,
        compiler_params=pltpu.CompilerParams(vmem_limit_bytes=PROJECT_VMEM),
        cost_estimate=pl.CostEstimate(
            flops=2 * rows * depth * size,
            bytes_accessed=2 * (rows * depth + depth * size + rows * size),
            transcendentals=0,
        ),
    )(values, weight)


def shards(
    hidden_in,
    q_latent,
    q_rope,
    cache_latent,
    cache_rope,
    lengths,
    value_up_weight,
    out_weight,
    norm_gain,
    route_ids,
    route_logits,
    gate_weight,
    up_weight,
    down_projection_weight,
):
    devices = lax.axis_size("expert")
    me = lax.axis_index("expert")
    nbits = devices.bit_length() - 1
    tokens_here = hidden_in.shape[0]
    model_width = hidden_in.shape[1]
    top_count = route_ids.shape[1]
    experts = devices // SHARDS
    stages = stage_bits(nbits)
    plans = chain_parts(model_width)
    orders = chain_orders(nbits)
    sum_stages = [[stages[0], *[stages[k] for k in order], stages[-1]] for order in orders]
    sigm = jax.nn.sigmoid(route_logits)
    route_weights = route_scale * sigm / jnp.sum(sigm, axis=1, keepdims=True)

    latent_out = attend(q_latent, q_rope, cache_latent, cache_rope, lengths)
    _, out_after, down_after, gate_after, up_after = lax.optimization_barrier(
        (latent_out, out_weight, down_projection_weight, gate_weight, up_weight)
    )
    both_near = jnp.concatenate([gate_after[0], up_after[0]], axis=1)
    out_near = [out_after[:, start : start + size] for start, size in plans]
    down_near = [down_after[0, :, start : start + size] for start, size in plans]
    by_head = lax.all_to_all(latent_out, "expert", split_axis=0, concat_axis=0, tiled=True)
    by_head, both_near, out_near, down_near = lax.optimization_barrier(
        (by_head, both_near, out_near, down_near)
    )
    heads_here = value_up_weight.shape[0]
    by_head = by_head.reshape(devices, heads_here, tokens_here, -1)
    head_values = jnp.einsum(
        "sqtg,qge->stqe", by_head, value_up_weight, preferred_element_type=f32
    ).astype(bf16)
    rows = devices * tokens_here
    head_values = head_values.reshape(rows, -1)
    at = jnp.arange(rows, dtype=jnp.int32)
    values = {}
    for order, its in zip(orders, sum_stages, strict=True):
        if tuple(order) not in values:
            source = row_sources(me, its, devices, tokens_here)
            shuffle = (source[:, None] == at[None, :]).astype(bf16)
            values[tuple(order)] = jnp.dot(
                shuffle, head_values, preferred_element_type=f32
            ).astype(bf16)

    chosen = route_ids[:, :, None] == jnp.arange(experts, dtype=jnp.int32)[None, None, :]
    shares = jnp.sum(jnp.where(chosen, route_weights[:, :, None], 0.0), axis=1)
    extra = jnp.concatenate(three_parts(shares), axis=1)
    extra = jnp.pad(extra, ((0, 0), (0, LANES - extra.shape[1])))
    dense = experts <= top_count

    residual = []
    for i, (start, size) in enumerate(plans):
        keep, send = project(values[tuple(orders[i])], out_near[i], 0, size)
        own, partners = halve(keep, send, sum_stages[i], devices)
        own = (own + hidden_in[:, start : start + size].astype(f32)).astype(bf16)
        both = jnp.concatenate([own, partners], axis=0)
        if dense and i + 1 == len(plans):
            beside = jnp.concatenate([extra, jnp.zeros_like(extra)], axis=0)
            both = jnp.concatenate([both, beside], axis=1)
        came = swap(both, stages[-1], devices)
        came = jnp.concatenate([came[tokens_here:], came[:tokens_here]], axis=0)
        residual.append(add32(both, came).astype(bf16))

    if not dense:
        return routed(
            jnp.concatenate(residual, axis=1)[:tokens_here],
            norm_gain,
            route_ids,
            route_weights,
            gate_weight,
            up_weight,
            down_projection_weight,
        )

    acts, squares, got = [0.0, 0.0], [0.0, 0.0], [None, None]
    for i, (start, size) in enumerate(plans):
        gain = norm_gain[start : start + size].astype(f32)
        for h, taken in enumerate(double(residual[i], stages[:-1], devices)):
            if i + 1 == len(plans):
                got[h] = taken[:, size:].astype(f32)
                taken = taken[:, :size]
            wide = taken.astype(f32)
            squares[h] = squares[h] + jnp.sum(wide * wide, axis=1, keepdims=True)
            acts[h] = acts[h] + jnp.dot(
                (wide * gain).astype(bf16),
                both_near[start : start + size],
                preferred_element_type=f32,
            )
    lane = jnp.arange(LANES, dtype=jnp.int32)
    own = (lane % experts == me // SHARDS) & (lane < 3 * experts)
    hidden = []
    for h in range(2):
        factor = lax.rsqrt(squares[h] / model_width + epsilon)
        share = jnp.sum(jnp.where(own[None, :], got[h], 0.0), axis=1, keepdims=True)
        gate_act, up_act = jnp.split(acts[h] * factor, 2, axis=1)
        hidden.append((jax.nn.silu(gate_act) * up_act * share).astype(bf16))
    hidden = jnp.concatenate(hidden, axis=0)
    out = []
    for i, ((start, size), base) in enumerate(zip(plans, residual, strict=True)):
        acts = hidden
        if orders[i] != sorted(orders[i]):
            move = np.eye(rows, dtype=np.float32)[place_rows(orders[i], rows)]
            acts = jnp.dot(jnp.asarray(move, bf16), hidden, preferred_element_type=f32).astype(bf16)
        keep, send = project(acts, down_near[i], 0, size)
        own, partners = halve(keep, send, sum_stages[i], devices)
        came = swap(partners, stages[-1], devices)
        total = base[:tokens_here, :size].astype(f32) + own + came.astype(f32)
        out.append(total.astype(bf16))
    return jnp.concatenate(out, axis=1)


def routed(
    residual, norm_gain, route_ids, route_weights, gate_weight, up_weight, down_projection_weight
):
    devices = lax.axis_size("expert")
    tokens_here, model_width = residual.shape
    top_count = route_ids.shape[1]
    experts = devices // SHARDS
    capacity = min(tokens_here, max(2, (tokens_here * top_count + experts - 1) // experts + 1))
    slot_count = experts * capacity
    slot_ids = slot_table(route_ids, experts, capacity)
    slot_range = jnp.arange(slot_count, dtype=jnp.int32)
    res32 = residual.astype(f32)
    normed = (
        res32
        * lax.rsqrt(jnp.mean(res32 * res32, axis=1, keepdims=True) + epsilon)
        * norm_gain.astype(f32)
    ).astype(bf16)
    placement = jnp.sum(
        (slot_ids[:, :, None] == slot_range[None, None, :]).astype(jnp.int32), axis=1
    ).astype(bf16)
    outgoing = jnp.einsum("tq,tw->qw", placement, normed, preferred_element_type=f32).astype(bf16)
    outgoing = jnp.broadcast_to(
        outgoing.reshape(experts, 1, capacity, model_width),
        (experts, SHARDS, capacity, model_width),
    )
    outgoing = outgoing.reshape(devices, capacity, model_width)
    received = lax.all_to_all(outgoing, "expert", split_axis=0, concat_axis=0, tiled=True)
    sources, item_count, feature_count = received.shape
    flattened = received.reshape(sources * item_count, feature_count)
    gate_act = jnp.dot(flattened, gate_weight[0], preferred_element_type=f32)
    up_act = jnp.dot(flattened, up_weight[0], preferred_element_type=f32)
    hidden = (jax.nn.silu(gate_act) * up_act).astype(bf16)
    piece_out = jnp.dot(hidden, down_projection_weight[0], preferred_element_type=f32).astype(bf16)
    returned_rows = lax.all_to_all(
        piece_out.reshape(sources, item_count, feature_count),
        "expert",
        split_axis=0,
        concat_axis=0,
        tiled=True,
    )
    combiner = jnp.sum(
        route_weights[:, :, None]
        * (slot_ids[:, :, None] == slot_range[None, None, :]).astype(f32),
        axis=1,
    )
    summed = jnp.sum(
        returned_rows.reshape(experts, SHARDS, capacity, model_width).astype(f32), axis=1
    ).reshape(slot_count, model_width)
    expert_sum = jnp.dot(combiner, summed, precision=lax.Precision.HIGHEST)
    return (res32 + expert_sum).astype(bf16)


def solution(mesh):
    placed = (
        P(("group", "expert"), None),
        P(("group", "expert"), None, None),
        P(("group", "expert"), None),
        P(("group", "expert"), None, None),
        P(("group", "expert"), None, None),
        P(("group", "expert")),
        P("expert", None, None),
        P("expert", None),
        P(),
        P(("group", "expert"), None),
        P(("group", "expert"), None),
        P("expert", None, None),
        P("expert", None, None),
        P("expert", None, None),
    )
    return jax.shard_map(
        shards, mesh=mesh, in_specs=placed, out_specs=P(("group", "expert"), None), check_vma=False
    )
```

```python
import functools

import jax
import jax.numpy as jnp
import numpy as np
from jax import lax
from jax.experimental import pallas as pl
from jax.experimental.pallas import tpu as pltpu
from jax.sharding import PartitionSpec as P

SHARDS = 8
LANES = 128
TILE = 128
CHAINS = 3
COLUMNS = 640
ATTEND_VMEM = 56 << 20
PROJECT_VMEM = 32 << 20


score_scale = 192.0 ** (-0.5)
epsilon = 1e-06
route_scale = 2.5
f32 = jnp.float32
bf16 = jnp.bfloat16


def slot_table(routes, experts, capacity):
    flattened = routes.reshape(-1)
    onehot = (flattened[:, None] == jnp.arange(experts, dtype=jnp.int32)[None, :]).astype(jnp.int32)
    before = jnp.cumsum(onehot, axis=0) - onehot
    ranking = jnp.sum(before * onehot, axis=1)
    return (flattened * capacity + ranking).reshape(routes.shape)


def stage_bits(nbits):
    low = list(range(nbits))
    high = [0, 2, 1, *low[3:]]
    return list(zip(low, high, strict=True))


def chain_parts(width):
    tiles = width // TILE
    sizes = [(tiles + i) // CHAINS * TILE for i in range(CHAINS)][::-1]
    return [(sum(sizes[:i]), size) for i, size in enumerate(sizes)]


def chain_orders(nbits):
    plain = list(range(1, nbits - 1))
    return [[3, 1, 2, *plain[3:]]] + [plain] * (CHAINS - 1)


def place_rows(order, rows):
    index = np.arange(rows).reshape(*(2,) * (len(order) + 1), -1)
    return index.transpose(0, *order, len(order) + 1).reshape(-1)


def swap(x, stage, devices):
    pairs = [(i, i ^ (1 << stage[i & 1])) for i in range(devices)]
    return lax.ppermute(x, "expert", pairs)


def row_sources(me, stages, devices, tokens_here):
    at = jnp.arange(devices * tokens_here, dtype=jnp.int32)
    place = at // tokens_here
    top = len(stages) - 1
    other = place >> top
    core = (me & 1) ^ other
    owner = me ^ other
    for step in range(1, len(stages)):
        bit = (place >> (top - step)) & 1
        owner = owner ^ jnp.where(core == 0, bit << stages[step][0], bit << stages[step][1])
    return owner * tokens_here + at % tokens_here


def add32(a, b):
    return a.astype(f32) + b.astype(f32)


def halve(keep, send, stages, devices):
    for step, stage in enumerate(stages[:-1]):
        came = swap(send, stage, devices)
        half = keep.shape[0] // 2
        send = add32(keep[half:], came[half:]).astype(bf16)
        keep = add32(keep[:half], came[:half])
        if step + 2 < len(stages):
            keep = keep.astype(bf16)
    return keep, send


def double(rows, stages, devices):
    for stage in stages[:0:-1]:
        rows = jnp.concatenate([rows, swap(rows, stage, devices)], axis=0)
    return rows, swap(rows, stages[0], devices)


def three_parts(x):
    parts = []
    for _ in range(3):
        part = lax.reduce_precision(x, 8, 7)
        parts.append(part.astype(bf16))
        x = x - part
    return parts


def attend_kernel(lengths_ref, latent_ref, rope_ref, keys_ref, turned_ref, out_ref, held_ref):
    step = pl.program_id(0)
    group = keys_ref.shape[0]
    for i in range(group):
        token = step * group + i
        keys = keys_ref[i]
        scores = lax.dot_general(
            latent_ref[i], keys, (((1,), (1,)), ((), ())), preferred_element_type=f32
        )
        scores = scores + jnp.dot(rope_ref[i], turned_ref[i], preferred_element_type=f32)
        scores = scores * score_scale
        column = lax.broadcasted_iota(jnp.int32, scores.shape, 1)
        scores = jnp.where(column < lengths_ref[token], scores, -jnp.inf)
        expd = jnp.exp(scores - jnp.max(scores, axis=1, keepdims=True))
        weights = (expd * (1.0 / jnp.sum(expd, axis=1, keepdims=True))).astype(bf16)
        held_ref[token] = jnp.dot(weights, keys, preferred_element_type=f32)

    @pl.when(step == pl.num_programs(0) - 1)
    def _():
        out_ref[...] = jnp.swapaxes(held_ref[...], 0, 1).astype(bf16)


def attend(q_latent, q_rope, cache_latent, cache_rope, lengths):
    tokens, heads, rank = q_latent.shape
    _, turned, cached = cache_rope.shape
    at = lambda i: (i, 0, 0)
    group = 2 if tokens % 2 == 0 else 1
    return pl.pallas_call(
        attend_kernel,
        grid=(tokens // group,),
        out_shape=jax.ShapeDtypeStruct((heads, tokens, rank), bf16),
        in_specs=[
            pl.BlockSpec(memory_space=pltpu.SMEM),
            pl.BlockSpec((group, heads, rank), at),
            pl.BlockSpec((group, heads, turned), at),
            pl.BlockSpec((group, cached, rank), at),
            pl.BlockSpec((group, turned, cached), at),
        ],
        out_specs=pl.BlockSpec((heads, tokens, rank), lambda i: (0, 0, 0)),
        scratch_shapes=[pltpu.VMEM((tokens, heads, rank), f32)],
        compiler_params=pltpu.CompilerParams(vmem_limit_bytes=ATTEND_VMEM),
        cost_estimate=pl.CostEstimate(
            flops=2 * tokens * heads * cached * (2 * rank + turned),
            bytes_accessed=2 * tokens * (2 * heads * rank + cached * (rank + turned)),
            transcendentals=tokens * heads * cached,
        ),
    )(lengths, q_latent, q_rope.reshape(tokens, heads, turned), cache_latent, cache_rope)


def project_kernel(start, values_ref, weight_ref, keep_ref, send_ref):
    half, size = keep_ref.shape
    for at in range(0, size, COLUMNS):
        width = min(COLUMNS, size - at)
        out = jnp.dot(
            values_ref[...],
            weight_ref[:, start + at : start + at + width],
            preferred_element_type=f32,
        ).astype(bf16)
        keep_ref[:, at : at + width] = out[:half]
        send_ref[:, at : at + width] = out[half:]


def project(values, weight, start, size):
    rows, depth = values.shape
    half = jax.ShapeDtypeStruct((rows // 2, size), bf16)
    return pl.pallas_call(
        functools.partial(project_kernel, start),
        out_shape=[half, half],
        in_specs=[pl.BlockSpec(memory_space=pltpu.VMEM)] * 2,
        out_specs=[pl.BlockSpec(memory_space=pltpu.VMEM)] * 2,
        compiler_params=pltpu.CompilerParams(vmem_limit_bytes=PROJECT_VMEM),
        cost_estimate=pl.CostEstimate(
            flops=2 * rows * depth * size,
            bytes_accessed=2 * (rows * depth + depth * size + rows * size),
            transcendentals=0,
        ),
    )(values, weight)


def shards(
    hidden_in,
    q_latent,
    q_rope,
    cache_latent,
    cache_rope,
    lengths,
    value_up_weight,
    out_weight,
    norm_gain,
    route_ids,
    route_logits,
    gate_weight,
    up_weight,
    down_projection_weight,
):
    devices = lax.axis_size("expert")
    me = lax.axis_index("expert")
    nbits = devices.bit_length() - 1
    tokens_here = hidden_in.shape[0]
    model_width = hidden_in.shape[1]
    top_count = route_ids.shape[1]
    experts = devices // SHARDS
    stages = stage_bits(nbits)
    plans = chain_parts(model_width)
    orders = chain_orders(nbits)
    sum_stages = [[stages[0], *[stages[k] for k in order], stages[-1]] for order in orders]
    sigm = jax.nn.sigmoid(route_logits)
    route_weights = route_scale * sigm / jnp.sum(sigm, axis=1, keepdims=True)

    latent_out = attend(q_latent, q_rope, cache_latent, cache_rope, lengths)
    _, out_after, down_after, gate_after, up_after = lax.optimization_barrier(
        (latent_out, out_weight, down_projection_weight, gate_weight, up_weight)
    )
    both_near = jnp.concatenate([gate_after[0], up_after[0]], axis=1)
    out_near = [out_after[:, start : start + size] for start, size in plans]
    down_near = [down_after[0, :, start : start + size] for start, size in plans]
    by_head = lax.all_to_all(latent_out, "expert", split_axis=0, concat_axis=0, tiled=True)
    by_head, both_near, out_near, down_near = lax.optimization_barrier(
        (by_head, both_near, out_near, down_near)
    )
    heads_here = value_up_weight.shape[0]
    by_head = by_head.reshape(devices, heads_here, tokens_here, -1)
    head_values = jnp.einsum(
        "sqtg,qge->stqe", by_head, value_up_weight, preferred_element_type=f32
    ).astype(bf16)
    rows = devices * tokens_here
    head_values = head_values.reshape(rows, -1)
    at = jnp.arange(rows, dtype=jnp.int32)
    values = {}
    for order, its in zip(orders, sum_stages, strict=True):
        if tuple(order) not in values:
            source = row_sources(me, its, devices, tokens_here)
            shuffle = (source[:, None] == at[None, :]).astype(bf16)
            values[tuple(order)] = jnp.dot(
                shuffle, head_values, preferred_element_type=f32
            ).astype(bf16)

    chosen = route_ids[:, :, None] == jnp.arange(experts, dtype=jnp.int32)[None, None, :]
    shares = jnp.sum(jnp.where(chosen, route_weights[:, :, None], 0.0), axis=1)
    extra = jnp.concatenate(three_parts(shares), axis=1)
    extra = jnp.pad(extra, ((0, 0), (0, LANES - extra.shape[1])))
    dense = experts <= top_count

    residual = []
    for i, (start, size) in enumerate(plans):
        keep, send = project(values[tuple(orders[i])], out_near[i], 0, size)
        own, partners = halve(keep, send, sum_stages[i], devices)
        own = (own + hidden_in[:, start : start + size].astype(f32)).astype(bf16)
        both = jnp.concatenate([own, partners], axis=0)
        if dense and i + 1 == len(plans):
            beside = jnp.concatenate([extra, jnp.zeros_like(extra)], axis=0)
            both = jnp.concatenate([both, beside], axis=1)
        came = swap(both, stages[-1], devices)
        came = jnp.concatenate([came[tokens_here:], came[:tokens_here]], axis=0)
        residual.append(add32(both, came).astype(bf16))

    if not dense:
        return routed(
            jnp.concatenate(residual, axis=1)[:tokens_here],
            norm_gain,
            route_ids,
            route_weights,
            gate_weight,
            up_weight,
            down_projection_weight,
        )

    acts, squares, got = [0.0, 0.0], [0.0, 0.0], [None, None]
    for i, (start, size) in enumerate(plans):
        gain = norm_gain[start : start + size].astype(f32)
        for h, taken in enumerate(double(residual[i], stages[:-1], devices)):
            if i + 1 == len(plans):
                got[h] = taken[:, size:].astype(f32)
                taken = taken[:, :size]
            wide = taken.astype(f32)
            squares[h] = squares[h] + jnp.sum(wide * wide, axis=1, keepdims=True)
            acts[h] = acts[h] + jnp.dot(
                (wide * gain).astype(bf16),
                both_near[start : start + size],
                preferred_element_type=f32,
            )
    lane = jnp.arange(LANES, dtype=jnp.int32)
    own = (lane % experts == me // SHARDS) & (lane < 3 * experts)
    hidden = []
    for h in range(2):
        factor = lax.rsqrt(squares[h] / model_width + epsilon)
        share = jnp.sum(jnp.where(own[None, :], got[h], 0.0), axis=1, keepdims=True)
        gate_act, up_act = jnp.split(acts[h] * factor, 2, axis=1)
        hidden.append((jax.nn.silu(gate_act) * up_act * share).astype(bf16))
    hidden = jnp.concatenate(hidden, axis=0)
    out = []
    for i, ((start, size), base) in enumerate(zip(plans, residual, strict=True)):
        acts = hidden
        if orders[i] != sorted(orders[i]):
            moved = place_rows(orders[i], rows)
            run = rows // 2 ** (len(orders[i]) + 1)
            acts = jnp.concatenate([hidden[k : k + run] for k in moved[::run].tolist()], axis=0)
        keep, send = project(acts, down_near[i], 0, size)
        own, partners = halve(keep, send, sum_stages[i], devices)
        came = swap(partners, stages[-1], devices)
        total = base[:tokens_here, :size].astype(f32) + own + came.astype(f32)
        out.append(total.astype(bf16))
    return jnp.concatenate(out, axis=1)


def routed(
    residual, norm_gain, route_ids, route_weights, gate_weight, up_weight, down_projection_weight
):
    devices = lax.axis_size("expert")
    tokens_here, model_width = residual.shape
    top_count = route_ids.shape[1]
    experts = devices // SHARDS
    capacity = min(tokens_here, max(2, (tokens_here * top_count + experts - 1) // experts + 1))
    slot_count = experts * capacity
    slot_ids = slot_table(route_ids, experts, capacity)
    slot_range = jnp.arange(slot_count, dtype=jnp.int32)
    res32 = residual.astype(f32)
    normed = (
        res32
        * lax.rsqrt(jnp.mean(res32 * res32, axis=1, keepdims=True) + epsilon)
        * norm_gain.astype(f32)
    ).astype(bf16)
    placement = jnp.sum(
        (slot_ids[:, :, None] == slot_range[None, None, :]).astype(jnp.int32), axis=1
    ).astype(bf16)
    outgoing = jnp.einsum("tq,tw->qw", placement, normed, preferred_element_type=f32).astype(bf16)
    outgoing = jnp.broadcast_to(
        outgoing.reshape(experts, 1, capacity, model_width),
        (experts, SHARDS, capacity, model_width),
    )
    outgoing = outgoing.reshape(devices, capacity, model_width)
    received = lax.all_to_all(outgoing, "expert", split_axis=0, concat_axis=0, tiled=True)
    sources, item_count, feature_count = received.shape
    flattened = received.reshape(sources * item_count, feature_count)
    gate_act = jnp.dot(flattened, gate_weight[0], preferred_element_type=f32)
    up_act = jnp.dot(flattened, up_weight[0], preferred_element_type=f32)
    hidden = (jax.nn.silu(gate_act) * up_act).astype(bf16)
    piece_out = jnp.dot(hidden, down_projection_weight[0], preferred_element_type=f32).astype(bf16)
    returned_rows = lax.all_to_all(
        piece_out.reshape(sources, item_count, feature_count),
        "expert",
        split_axis=0,
        concat_axis=0,
        tiled=True,
    )
    combiner = jnp.sum(
        route_weights[:, :, None]
        * (slot_ids[:, :, None] == slot_range[None, None, :]).astype(f32),
        axis=1,
    )
    summed = jnp.sum(
        returned_rows.reshape(experts, SHARDS, capacity, model_width).astype(f32), axis=1
    ).reshape(slot_count, model_width)
    expert_sum = jnp.dot(combiner, summed, precision=lax.Precision.HIGHEST)
    return (res32 + expert_sum).astype(bf16)


def solution(mesh):
    placed = (
        P(("group", "expert"), None),
        P(("group", "expert"), None, None),
        P(("group", "expert"), None),
        P(("group", "expert"), None, None),
        P(("group", "expert"), None, None),
        P(("group", "expert")),
        P("expert", None, None),
        P("expert", None),
        P(),
        P(("group", "expert"), None),
        P(("group", "expert"), None),
        P("expert", None, None),
        P("expert", None, None),
        P("expert", None, None),
    )
    return jax.shard_map(
        shards, mesh=mesh, in_specs=placed, out_specs=P(("group", "expert"), None), check_vma=False
    )
```

```python
import functools

import jax
import jax.numpy as jnp
import numpy as np
from jax import lax
from jax.experimental import pallas as pl
from jax.experimental.pallas import tpu as pltpu
from jax.sharding import PartitionSpec as P

SHARDS = 8
LANES = 128
TILE = 128
CHAINS = 3
COLUMNS = 640
ATTEND_VMEM = 56 << 20
PROJECT_VMEM = 32 << 20


score_scale = 192.0 ** (-0.5)
epsilon = 1e-06
route_scale = 2.5
f32 = jnp.float32
bf16 = jnp.bfloat16


def slot_table(routes, experts, capacity):
    flattened = routes.reshape(-1)
    onehot = (flattened[:, None] == jnp.arange(experts, dtype=jnp.int32)[None, :]).astype(jnp.int32)
    before = jnp.cumsum(onehot, axis=0) - onehot
    ranking = jnp.sum(before * onehot, axis=1)
    return (flattened * capacity + ranking).reshape(routes.shape)


def stage_bits(nbits):
    low = list(range(nbits))
    high = [0, 2, 1, *low[3:]]
    return list(zip(low, high, strict=True))


def chain_parts(width):
    tiles = width // TILE
    sizes = [(tiles + i) // CHAINS * TILE for i in range(CHAINS)][::-1]
    return [(sum(sizes[:i]), size) for i, size in enumerate(sizes)]


def chain_orders(nbits):
    plain = list(range(1, nbits - 1))
    return [[3, 1, 2, *plain[3:]]] + [plain] * (CHAINS - 1)


def place_rows(order, rows):
    index = np.arange(rows).reshape(*(2,) * (len(order) + 1), -1)
    return index.transpose(0, *order, len(order) + 1).reshape(-1)


def swap(x, stage, devices):
    pairs = [(i, i ^ (1 << stage[i & 1])) for i in range(devices)]
    return lax.ppermute(x, "expert", pairs)


def row_sources(me, stages, devices, tokens_here):
    at = jnp.arange(devices * tokens_here, dtype=jnp.int32)
    place = at // tokens_here
    top = len(stages) - 1
    other = place >> top
    core = (me & 1) ^ other
    owner = me ^ other
    for step in range(1, len(stages)):
        bit = (place >> (top - step)) & 1
        owner = owner ^ jnp.where(core == 0, bit << stages[step][0], bit << stages[step][1])
    return owner * tokens_here + at % tokens_here


def add32(a, b):
    return a.astype(f32) + b.astype(f32)


def halve(keep, send, stages, devices):
    for step, stage in enumerate(stages[:-1]):
        came = swap(send, stage, devices)
        half = keep.shape[0] // 2
        send = add32(keep[half:], came[half:]).astype(bf16)
        keep = add32(keep[:half], came[:half])
        if step + 2 < len(stages):
            keep = keep.astype(bf16)
    return keep, send


def double(rows, stages, devices):
    for stage in stages[:0:-1]:
        rows = jnp.concatenate([rows, swap(rows, stage, devices)], axis=0)
    return rows, swap(rows, stages[0], devices)


def three_parts(x):
    parts = []
    for _ in range(3):
        part = lax.reduce_precision(x, 8, 7)
        parts.append(part.astype(bf16))
        x = x - part
    return parts


def attend_kernel(lengths_ref, latent_ref, rope_ref, keys_ref, turned_ref, out_ref, held_ref):
    step = pl.program_id(0)
    group = keys_ref.shape[0]
    for i in range(group):
        token = step * group + i
        keys = keys_ref[i]
        scores = lax.dot_general(
            latent_ref[i], keys, (((1,), (1,)), ((), ())), preferred_element_type=f32
        )
        scores = scores + jnp.dot(rope_ref[i], turned_ref[i], preferred_element_type=f32)
        scores = scores * score_scale
        column = lax.broadcasted_iota(jnp.int32, scores.shape, 1)
        scores = jnp.where(column < lengths_ref[token], scores, -jnp.inf)
        expd = jnp.exp(scores - jnp.max(scores, axis=1, keepdims=True))
        weights = (expd * (1.0 / jnp.sum(expd, axis=1, keepdims=True))).astype(bf16)
        held_ref[token] = jnp.dot(weights, keys, preferred_element_type=f32)

    @pl.when(step == pl.num_programs(0) - 1)
    def _():
        out_ref[...] = jnp.swapaxes(held_ref[...], 0, 1).astype(bf16)


def attend(q_latent, q_rope, cache_latent, cache_rope, lengths):
    tokens, heads, rank = q_latent.shape
    _, turned, cached = cache_rope.shape
    at = lambda i: (i, 0, 0)
    group = 2 if tokens % 2 == 0 else 1
    return pl.pallas_call(
        attend_kernel,
        grid=(tokens // group,),
        out_shape=jax.ShapeDtypeStruct((heads, tokens, rank), bf16),
        in_specs=[
            pl.BlockSpec(memory_space=pltpu.SMEM),
            pl.BlockSpec((group, heads, rank), at),
            pl.BlockSpec((group, heads, turned), at),
            pl.BlockSpec((group, cached, rank), at),
            pl.BlockSpec((group, turned, cached), at),
        ],
        out_specs=pl.BlockSpec((heads, tokens, rank), lambda i: (0, 0, 0)),
        scratch_shapes=[pltpu.VMEM((tokens, heads, rank), f32)],
        compiler_params=pltpu.CompilerParams(vmem_limit_bytes=ATTEND_VMEM),
        cost_estimate=pl.CostEstimate(
            flops=2 * tokens * heads * cached * (2 * rank + turned),
            bytes_accessed=2 * tokens * (2 * heads * rank + cached * (rank + turned)),
            transcendentals=tokens * heads * cached,
        ),
    )(lengths, q_latent, q_rope.reshape(tokens, heads, turned), cache_latent, cache_rope)


def project_kernel(start, values_ref, weight_ref, keep_ref, send_ref):
    half, size = keep_ref.shape
    for at in range(0, size, COLUMNS):
        width = min(COLUMNS, size - at)
        out = jnp.dot(
            values_ref[...],
            weight_ref[:, start + at : start + at + width],
            preferred_element_type=f32,
        ).astype(bf16)
        keep_ref[:, at : at + width] = out[:half]
        send_ref[:, at : at + width] = out[half:]


def project(values, weight, start, size):
    rows, depth = values.shape
    half = jax.ShapeDtypeStruct((rows // 2, size), bf16)
    return pl.pallas_call(
        functools.partial(project_kernel, start),
        out_shape=[half, half],
        in_specs=[pl.BlockSpec(memory_space=pltpu.VMEM)] * 2,
        out_specs=[pl.BlockSpec(memory_space=pltpu.VMEM)] * 2,
        compiler_params=pltpu.CompilerParams(vmem_limit_bytes=PROJECT_VMEM),
        cost_estimate=pl.CostEstimate(
            flops=2 * rows * depth * size,
            bytes_accessed=2 * (rows * depth + depth * size + rows * size),
            transcendentals=0,
        ),
    )(values, weight)


def shards(
    hidden_in,
    q_latent,
    q_rope,
    cache_latent,
    cache_rope,
    lengths,
    value_up_weight,
    out_weight,
    norm_gain,
    route_ids,
    route_logits,
    gate_weight,
    up_weight,
    down_projection_weight,
):
    devices = lax.axis_size("expert")
    me = lax.axis_index("expert")
    nbits = devices.bit_length() - 1
    tokens_here = hidden_in.shape[0]
    model_width = hidden_in.shape[1]
    top_count = route_ids.shape[1]
    experts = devices // SHARDS
    stages = stage_bits(nbits)
    plans = chain_parts(model_width)
    orders = chain_orders(nbits)
    sum_stages = [[stages[0], *[stages[k] for k in order], stages[-1]] for order in orders]
    sigm = jax.nn.sigmoid(route_logits)
    route_weights = route_scale * sigm / jnp.sum(sigm, axis=1, keepdims=True)

    latent_out = attend(q_latent, q_rope, cache_latent, cache_rope, lengths)
    _, out_after, down_after, gate_after, up_after = lax.optimization_barrier(
        (latent_out, out_weight, down_projection_weight, gate_weight, up_weight)
    )
    both_near = jnp.concatenate([gate_after[0], up_after[0]], axis=1)
    out_near = [out_after[:, start : start + size] for start, size in plans]
    down_near = [down_after[0, :, start : start + size] for start, size in plans]
    by_head = lax.all_to_all(latent_out, "expert", split_axis=0, concat_axis=0, tiled=True)
    by_head, both_near, out_near, down_near = lax.optimization_barrier(
        (by_head, both_near, out_near, down_near)
    )
    heads_here = value_up_weight.shape[0]
    by_head = by_head.reshape(devices, heads_here, tokens_here, -1)
    head_values = jnp.einsum(
        "sqtg,qge->stqe", by_head, value_up_weight, preferred_element_type=f32
    ).astype(bf16)
    rows = devices * tokens_here
    head_values = head_values.reshape(rows, -1)
    at = jnp.arange(rows, dtype=jnp.int32)
    values = {}
    for order, its in zip(orders, sum_stages, strict=True):
        if tuple(order) not in values:
            source = row_sources(me, its, devices, tokens_here)
            shuffle = (source[:, None] == at[None, :]).astype(bf16)
            values[tuple(order)] = jnp.dot(
                shuffle, head_values, preferred_element_type=f32
            ).astype(bf16)

    chosen = route_ids[:, :, None] == jnp.arange(experts, dtype=jnp.int32)[None, None, :]
    shares = jnp.sum(jnp.where(chosen, route_weights[:, :, None], 0.0), axis=1)
    extra = jnp.concatenate(three_parts(shares), axis=1)
    extra = jnp.pad(extra, ((0, 0), (0, LANES - extra.shape[1])))
    dense = experts <= top_count

    residual = []
    for i, (start, size) in enumerate(plans):
        keep, send = project(values[tuple(orders[i])], out_near[i], 0, size)
        own, partners = halve(keep, send, sum_stages[i], devices)
        own = (own + hidden_in[:, start : start + size].astype(f32)).astype(bf16)
        both = jnp.concatenate([own, partners], axis=0)
        if dense and i + 1 == len(plans):
            beside = jnp.concatenate([extra, jnp.zeros_like(extra)], axis=0)
            both = jnp.concatenate([both, beside], axis=1)
        came = swap(both, stages[-1], devices)
        came = jnp.concatenate([came[tokens_here:], came[:tokens_here]], axis=0)
        residual.append(add32(both, came).astype(bf16))

    if not dense:
        return routed(
            jnp.concatenate(residual, axis=1)[:tokens_here],
            norm_gain,
            route_ids,
            route_weights,
            gate_weight,
            up_weight,
            down_projection_weight,
        )

    acts, squares, got = [0.0, 0.0], [0.0, 0.0], [None, None]
    for i, (start, size) in enumerate(plans):
        gain = norm_gain[start : start + size].astype(f32)
        for h, taken in enumerate(double(residual[i], stages[:-1], devices)):
            if i + 1 == len(plans):
                got[h] = taken[:, size:].astype(f32)
                taken = taken[:, :size]
            wide = taken.astype(f32)
            squares[h] = squares[h] + jnp.sum(wide * wide, axis=1, keepdims=True)
            acts[h] = acts[h] + jnp.dot(
                (wide * gain).astype(bf16),
                both_near[start : start + size],
                preferred_element_type=f32,
            )
    lane = jnp.arange(LANES, dtype=jnp.int32)
    own = (lane % experts == me // SHARDS) & (lane < 3 * experts)
    hidden = []
    for h in range(2):
        factor = lax.rsqrt(squares[h] / model_width + epsilon)
        share = jnp.sum(jnp.where(own[None, :], got[h], 0.0), axis=1, keepdims=True)
        gate_act, up_act = jnp.split(acts[h] * factor, 2, axis=1)
        hidden.append((jax.nn.silu(gate_act) * up_act * share).astype(bf16))
    hidden = jnp.concatenate(hidden, axis=0)
    out = []
    for i, ((start, size), base) in list(enumerate(zip(plans, residual, strict=True)))[::-1]:
        acts = hidden
        if orders[i] != sorted(orders[i]):
            moved = place_rows(orders[i], rows)
            run = rows // 2 ** (len(orders[i]) + 1)
            acts = jnp.concatenate([hidden[k : k + run] for k in moved[::run].tolist()], axis=0)
        keep, send = project(acts, down_near[i], 0, size)
        own, partners = halve(keep, send, sum_stages[i], devices)
        came = swap(partners, stages[-1], devices)
        total = base[:tokens_here, :size].astype(f32) + own + came.astype(f32)
        out.append(total.astype(bf16))
    return jnp.concatenate(out[::-1], axis=1)


def routed(
    residual, norm_gain, route_ids, route_weights, gate_weight, up_weight, down_projection_weight
):
    devices = lax.axis_size("expert")
    tokens_here, model_width = residual.shape
    top_count = route_ids.shape[1]
    experts = devices // SHARDS
    capacity = min(tokens_here, max(2, (tokens_here * top_count + experts - 1) // experts + 1))
    slot_count = experts * capacity
    slot_ids = slot_table(route_ids, experts, capacity)
    slot_range = jnp.arange(slot_count, dtype=jnp.int32)
    res32 = residual.astype(f32)
    normed = (
        res32
        * lax.rsqrt(jnp.mean(res32 * res32, axis=1, keepdims=True) + epsilon)
        * norm_gain.astype(f32)
    ).astype(bf16)
    placement = jnp.sum(
        (slot_ids[:, :, None] == slot_range[None, None, :]).astype(jnp.int32), axis=1
    ).astype(bf16)
    outgoing = jnp.einsum("tq,tw->qw", placement, normed, preferred_element_type=f32).astype(bf16)
    outgoing = jnp.broadcast_to(
        outgoing.reshape(experts, 1, capacity, model_width),
        (experts, SHARDS, capacity, model_width),
    )
    outgoing = outgoing.reshape(devices, capacity, model_width)
    received = lax.all_to_all(outgoing, "expert", split_axis=0, concat_axis=0, tiled=True)
    sources, item_count, feature_count = received.shape
    flattened = received.reshape(sources * item_count, feature_count)
    gate_act = jnp.dot(flattened, gate_weight[0], preferred_element_type=f32)
    up_act = jnp.dot(flattened, up_weight[0], preferred_element_type=f32)
    hidden = (jax.nn.silu(gate_act) * up_act).astype(bf16)
    piece_out = jnp.dot(hidden, down_projection_weight[0], preferred_element_type=f32).astype(bf16)
    returned_rows = lax.all_to_all(
        piece_out.reshape(sources, item_count, feature_count),
        "expert",
        split_axis=0,
        concat_axis=0,
        tiled=True,
    )
    combiner = jnp.sum(
        route_weights[:, :, None]
        * (slot_ids[:, :, None] == slot_range[None, None, :]).astype(f32),
        axis=1,
    )
    summed = jnp.sum(
        returned_rows.reshape(experts, SHARDS, capacity, model_width).astype(f32), axis=1
    ).reshape(slot_count, model_width)
    expert_sum = jnp.dot(combiner, summed, precision=lax.Precision.HIGHEST)
    return (res32 + expert_sum).astype(bf16)


def solution(mesh):
    placed = (
        P(("group", "expert"), None),
        P(("group", "expert"), None, None),
        P(("group", "expert"), None),
        P(("group", "expert"), None, None),
        P(("group", "expert"), None, None),
        P(("group", "expert")),
        P("expert", None, None),
        P("expert", None),
        P(),
        P(("group", "expert"), None),
        P(("group", "expert"), None),
        P("expert", None, None),
        P("expert", None, None),
        P("expert", None, None),
    )
    return jax.shard_map(
        shards, mesh=mesh, in_specs=placed, out_specs=P(("group", "expert"), None), check_vma=False
    )
```
